256 devices in a mesh: row: 8 (over z), col: 32 (over y, x, core).
Axes of the slice: x: 4, y: 4, z: 8, core: 2. Of those that a mesh axis runs over, the one named last changes fastest.
Arguments:
- features: bfloat16 [65536, 128], P(('col', 'row')), may hold values from -6 to 6
- weight: bfloat16 [128, 256], replicated, may hold values from -0.5 to 0.5
- adj_tiles: bfloat16 [8, 32, 320, 128, 128], P('row', 'col'), may hold values from -0.078125 to 0.078125
- tile_rows: int32 [8, 32, 320], P('row', 'col'), may hold values from 0 to 63, as said below
- tile_cols: int32 [8, 32, 320], P('row', 'col'), may hold values from 0 to 15
- tile_count: int32 [8, 32], P('row', 'col'), may hold values from 20 to 320, as said below
- cotangent: bfloat16 [65536, 256], P(('row', 'col')), may hold values from -6 to 6
Outputs:
- hidden: bfloat16 [65536, 256], P(('row', 'col'))
- input_grad: bfloat16 [65536, 128], P(('col', 'row'))
- weight_grad: float32 [128, 256], replicated
The draws below stay inside these ranges and needn't reach their ends.
Inputs may be any that keep to these rules, and one draw needn't show every extreme that they name: Within one block the 320 slots name distinct tile places (tile_rows, tile_cols). `tile_count`: in every draw some block uses all 320 slots.
All inputs are finite; a program needn't handle non-finite values.
Results may differ from the reference program's by a relative error of at most 0.027.
Values may be sent and summed in bfloat16 or wider, within the bound.
No kernel may reach another device: no remote copies, remote signals or barrier semaphores. Data moves between devices by JAX's collectives and lax.ppermute only.
A program may use at most 128 MiB of HBM per device.

```python
import jax
import jax.numpy as jnp
from jax import lax

FIN = 128
HID = 256
TILE = 128
SLOTS = 5
ROW_TILES = 64
COL_TILES = 16
MAXT = 320
NODES = 65536
N_ROW = 8
N_COL = 32


def tile_places(key):
    subkeys = jax.random.split(key, N_ROW * N_COL)
    places = jax.vmap(lambda subkey: jax.random.permutation(subkey, ROW_TILES * COL_TILES)[:MAXT])(subkeys)
    return places.reshape(N_ROW, N_COL, MAXT).astype(jnp.int32)


def draw_tile_rows(key, part):
    places = tile_places(key)
    return (places // COL_TILES).astype(jnp.int32)


def draw_tile_cols(key, part):
    places = tile_places(key)
    return (places % COL_TILES).astype(jnp.int32)


def draw_tile_count(key, part):
    key = jax.random.fold_in(key, 7)
    level_key, busy_key = jax.random.split(key)
    lowest = max(MAXT // 16, 1)
    level = jax.random.randint(level_key, (N_ROW * N_COL,), 0, 256)
    counts = lowest + (MAXT - lowest) * level * level // 65025
    busiest = jax.random.randint(busy_key, (), 0, N_ROW * N_COL)
    counts = counts.at[busiest].set(MAXT)
    return counts.reshape(N_ROW, N_COL).astype(jnp.int32)


def shard_levels(own_key, shape, cuts, low, high):
    gain, own = 1.0, jax.random.fold_in(own_key, 6)
    for axis_at, shards_of in cuts:
        heights = jnp.exp(jax.random.uniform(jax.random.fold_in(own, axis_at), (shards_of,), jnp.float32, low / len(cuts), high / len(cuts)))
        gain = gain * jnp.repeat(heights, shape[axis_at] // shards_of).reshape([-1 if axis == axis_at else 1 for axis in range(len(shape))])
    return gain


def centred(key, extent, scale, limit, cuts=(), held_as=jnp.bfloat16):
    result = scale * jax.random.normal(key, extent, jnp.float32)
    if cuts:
        result = result * shard_levels(key, extent, cuts, -0.22, 0.18)
    return jnp.clip(result, -limit, limit).astype(held_as)


def setup_inputs(seed: int = 0) -> dict:
    streams_of = jax.random.split(jax.random.key(seed), 8)
    features = centred(streams_of[0], (NODES, FIN), 1.0, 6.0, ((0, 256),))
    weight = centred(streams_of[1], (FIN, HID), FIN ** -0.5, 0.5)
    adj_tiles = centred(streams_of[2], (N_ROW, N_COL, MAXT, TILE, TILE), (TILE * SLOTS * N_COL // 3) ** -0.5, 0.078125, ((0, 8), (1, 32)))
    tile_rows = draw_tile_rows(jax.random.fold_in(streams_of[7], 71), 0)
    tile_cols = draw_tile_cols(jax.random.fold_in(streams_of[7], 71), 0)
    tile_count = draw_tile_count(jax.random.fold_in(streams_of[7], 71), 0)
    cotangent = centred(streams_of[6], (NODES, HID), 1.0, 6.0, ((0, 256),))
    return {"features": features, "weight": weight, "adj_tiles": adj_tiles, "tile_rows": tile_rows, "tile_cols": tile_cols, "tile_count": tile_count, "cotangent": cotangent}


def forward_partial(blocks, row_list, col_list, live_count, x_panel):
    live_mask = (jnp.arange(MAXT, dtype=jnp.int32) < live_count).astype(jnp.float32)

    def advance(running, slot_group):
        first_slot = slot_group * ROW_TILES
        block_group = lax.dynamic_slice_in_dim(blocks, first_slot, ROW_TILES, 0)
        row_group = lax.dynamic_slice_in_dim(row_list, first_slot, ROW_TILES, 0)
        col_group = lax.dynamic_slice_in_dim(col_list, first_slot, ROW_TILES, 0)
        mask_group = lax.dynamic_slice_in_dim(live_mask, first_slot, ROW_TILES, 0)
        picked = jnp.take(x_panel, col_group, axis=0)
        product = jnp.einsum('kij,kjf->kif', block_group.astype(jnp.float32), picked.astype(jnp.float32))
        product = product * mask_group[:, None, None]
        return (running + jax.ops.segment_sum(product, row_group, num_segments=ROW_TILES), None)
    initial = jnp.zeros((ROW_TILES, TILE, FIN), jnp.float32)
    running, _ = lax.scan(advance, initial, jnp.arange(SLOTS, dtype=jnp.int32))
    return running

def backward_partial(blocks, row_list, col_list, live_count, grad_panel):
    live_mask = (jnp.arange(MAXT, dtype=jnp.int32) < live_count).astype(jnp.float32)

    def advance(running, slot_group):
        first_slot = slot_group * ROW_TILES
        block_group = lax.dynamic_slice_in_dim(blocks, first_slot, ROW_TILES, 0)
        row_group = lax.dynamic_slice_in_dim(row_list, first_slot, ROW_TILES, 0)
        col_group = lax.dynamic_slice_in_dim(col_list, first_slot, ROW_TILES, 0)
        mask_group = lax.dynamic_slice_in_dim(live_mask, first_slot, ROW_TILES, 0)
        picked = jnp.take(grad_panel, row_group, axis=0)
        product = jnp.einsum('kij,kif->kjf', block_group.astype(jnp.float32), picked.astype(jnp.float32))
        product = product * mask_group[:, None, None]
        return (running + jax.ops.segment_sum(product, col_group, num_segments=COL_TILES), None)
    initial = jnp.zeros((COL_TILES, TILE, FIN), jnp.float32)
    running, _ = lax.scan(advance, initial, jnp.arange(SLOTS, dtype=jnp.int32))
    return running

def reference(features, weight, adj_tiles, tile_rows, tile_cols, tile_count, cotangent):
    x_blocks = features.reshape(N_COL, COL_TILES, TILE, FIN)

    def row_block(row_index):

        def visit(running, col_index):
            part_sum = forward_partial(adj_tiles[row_index, col_index], tile_rows[row_index, col_index], tile_cols[row_index, col_index], tile_count[row_index, col_index], x_blocks[col_index])
            return (running + part_sum, None)
        initial = jnp.zeros((ROW_TILES, TILE, FIN), jnp.float32)
        running, _ = lax.scan(visit, initial, jnp.arange(N_COL, dtype=jnp.int32))
        return running
    aggregated = lax.map(row_block, jnp.arange(N_ROW, dtype=jnp.int32)).reshape(NODES, FIN)
    pre_act = jnp.dot(aggregated, weight.astype(jnp.float32), precision=lax.Precision.HIGHEST)
    activated, pullback = jax.vjp(lambda values: jax.nn.gelu(values, approximate=True), pre_act)
    hidden = activated.astype(jnp.bfloat16)
    act_grad = pullback(cotangent.astype(jnp.float32))[0]
    weight_grad = jnp.dot(aggregated.T, act_grad, precision=lax.Precision.HIGHEST) * NODES ** (-0.5)
    act_low = act_grad.astype(jnp.bfloat16)
    agg_grad = jnp.dot(act_low, weight.T, preferred_element_type=jnp.float32).astype(jnp.bfloat16)
    grad_blocks = agg_grad.reshape(N_ROW, ROW_TILES, TILE, FIN)

    def col_block(col_index):

        def visit(running, row_index):
            part_sum = backward_partial(adj_tiles[row_index, col_index], tile_rows[row_index, col_index], tile_cols[row_index, col_index], tile_count[row_index, col_index], grad_blocks[row_index])
            return (running + part_sum, None)
        initial = jnp.zeros((COL_TILES, TILE, FIN), jnp.float32)
        running, _ = lax.scan(visit, initial, jnp.arange(N_ROW, dtype=jnp.int32))
        return running
    input_grad = lax.map(col_block, jnp.arange(N_COL, dtype=jnp.int32)).reshape(NODES, FIN).astype(jnp.bfloat16)
    return (hidden, input_grad, weight_grad)
```

```python
import jax
import jax.numpy as jnp
from jax import lax
from jax.experimental import pallas as pl
from jax.experimental.pallas import tpu as pltpu
from jax.sharding import Mesh, PartitionSpec as P

F32, BF16 = jnp.float32, jnp.bfloat16
HIGHEST = lax.Precision.HIGHEST
UNROLL = 8
WROWS = 16
SMEM = pl.BlockSpec(memory_space=pltpu.SMEM)
VMEM = pl.BlockSpec(memory_space=pltpu.VMEM)


def in_vmem(value):
    return pltpu.with_memory_space_constraint(value, pltpu.VMEM)


def params(mebibytes):
    return pltpu.CompilerParams(vmem_limit_bytes=mebibytes * 2**20)


def forward_kernel(meta, rows, cols, tiles, panel, keep, send, acc):
    live, core = meta[0], meta[1]
    trash = acc.shape[0] - 1
    size = tiles.shape[-1]
    per_peer = keep.shape[1] // size
    acc[...] = jnp.zeros_like(acc)

    def group(step, carry):
        products, targets = [], []
        for offset in range(UNROLL):
            slot = step * UNROLL + offset
            targets.append(jnp.where(slot < live, rows[slot], trash))
            products.append(jnp.dot(tiles[slot], panel[cols[slot]], preferred_element_type=F32))
        for target, product in zip(targets, products):
            acc[target] += product
        return carry

    lax.fori_loop(0, pl.cdiv(live, UNROLL), group, 0)

    def emit(peer, carry):
        for part in range(per_peer):
            spot = pl.ds(part * size, size)
            keep[peer, spot] = acc[(2 * peer + core) * per_peer + part].astype(BF16)
            send[peer, spot] = acc[(2 * peer + 1 - core) * per_peer + part].astype(BF16)
        return carry

    lax.fori_loop(0, keep.shape[0], emit, 0)


def middle_kernel(parts, weight, cotangent, hidden, payload):
    own = hidden.shape[0]
    peers = parts.shape[0]
    feat = weight.shape[0]
    agg = parts[0].astype(F32)
    for peer in range(1, peers):
        agg += parts[peer].astype(F32)
    wide = weight[...].astype(F32)
    pre = jnp.dot(agg, wide, precision=HIGHEST, preferred_element_type=F32)
    slope, cubic = 0.7978845608028654, 0.044715
    square = pre * pre
    curve = jnp.tanh(slope * pre * (1.0 + cubic * square))
    cdf = 0.5 * (1.0 + curve)
    hidden[...] = (pre * cdf).astype(BF16)
    rate = cdf + 0.5 * pre * (1.0 - curve * curve) * (slope * (1.0 + 3.0 * cubic * square))
    act = cotangent[...].astype(F32) * rate
    local = lax.dot_general(
        agg, act, (((0,), (0,)), ((), ())), precision=HIGHEST, preferred_element_type=F32
    )
    grad = lax.dot_general(
        act.astype(BF16), weight[...], (((1,), (1,)), ((), ())), preferred_element_type=F32
    ).astype(BF16)
    per_half = feat // WROWS
    for peer in range(peers):
        payload[peer, :own] = grad
        half, chunk = divmod(peer, per_half)
        payload[peer, own:] = local[
            chunk * WROWS : (chunk + 1) * WROWS, half * feat : (half + 1) * feat
        ].astype(BF16)


def backward_kernel(meta, rows, cols, tiles, mine, other, out, grads, acc):
    live, core = meta[0], meta[1]
    size = tiles.shape[-1]
    trash = acc.shape[0] - 1
    peers = mine.shape[0]
    own = mine.shape[1] - WROWS
    per_peer = own // size
    acc[...] = jnp.zeros_like(acc)

    def place(peer, carry):
        for part in range(per_peer):
            spot = pl.ds(part * size, size)
            grads[(2 * peer + core) * per_peer + part] = mine[peer, spot]
            grads[(2 * peer + 1 - core) * per_peer + part] = other[peer, spot]
        return carry

    lax.fori_loop(0, peers, place, 0)

    def group(step, carry):
        products, targets = [], []
        for offset in range(UNROLL):
            slot = step * UNROLL + offset
            targets.append(jnp.where(slot < live, cols[slot], trash))
            products.append(
                lax.dot_general(
                    tiles[slot],
                    grads[rows[slot]],
                    (((0,), (0,)), ((), ())),
                    preferred_element_type=F32,
                )
            )
        for target, product in zip(targets, products):
            acc[target] += product
        return carry

    lax.fori_loop(0, pl.cdiv(live, UNROLL), group, 0)
    chunk = jnp.zeros((WROWS, size), F32)
    for peer in range(peers):
        chunk += mine[peer, own:].astype(F32) + other[peer, own:].astype(F32)
    for peer in range(out.shape[0]):
        for part in range(per_peer):
            out[peer, part * size : (part + 1) * size] = acc[peer * per_peer + part].astype(BF16)
        out[peer, own:] = chunk.astype(BF16)


def final_kernel(parts, grad, chunk, scale):
    total = parts[0].astype(F32)
    for peer in range(1, parts.shape[0]):
        total += parts[peer].astype(F32)
    own = grad.shape[0]
    grad[...] = total[:own].astype(BF16)
    chunk[...] = total[own:] * scale


def per_device(features, weight, adj_tiles, tile_rows, tile_cols, tile_count, cotangent):
    own, feat = features.shape
    n_row = lax.axis_size("row")
    peers = lax.axis_size("y") * lax.axis_size("x")
    slots, size = adj_tiles.shape[2], adj_tiles.shape[-1]
    row_tiles = own * peers * 2 // size
    col_tiles = own * n_row // size
    tiles = in_vmem(adj_tiles.reshape(slots, size, size))
    rows, cols = tile_rows.reshape(slots), tile_cols.reshape(slots)
    meta = jnp.stack([tile_count.reshape(()), lax.axis_index("core").astype(jnp.int32)])
    swap = [(0, 1), (1, 0)]
    yx = ("y", "x")

    spread = jnp.broadcast_to(features[None], (n_row, own, feat))
    panel = lax.all_to_all(spread, "row", 0, 0, tiled=True).reshape(col_tiles, size, feat)
    keep, send = pl.pallas_call(
        forward_kernel,
        out_shape=[jax.ShapeDtypeStruct((peers, own, feat), BF16)] * 2,
        in_specs=[SMEM, SMEM, SMEM, VMEM, VMEM],
        out_specs=[VMEM, VMEM],
        scratch_shapes=[pltpu.VMEM((row_tiles + 1, size, feat), F32)],
        compiler_params=params(24),
        name="forward",
    )(meta, rows, cols, tiles, panel)
    got = lax.ppermute(send, "core", swap)
    paired = (keep.astype(F32) + got.astype(F32)).astype(BF16)
    parts = lax.all_to_all(paired, yx, 0, 0, tiled=True)
    hidden, payload = pl.pallas_call(
        middle_kernel,
        out_shape=[
            jax.ShapeDtypeStruct(cotangent.shape, BF16),
            jax.ShapeDtypeStruct((peers, own + WROWS, feat), BF16),
        ],
        in_specs=[VMEM, VMEM, VMEM],
        out_specs=[VMEM, VMEM],
        compiler_params=params(24),
        name="middle",
    )(parts, weight, cotangent)
    mine = lax.all_to_all(payload, yx, 0, 0, tiled=True)
    other = lax.ppermute(mine, "core", swap)
    col_partial = pl.pallas_call(
        backward_kernel,
        out_shape=jax.ShapeDtypeStruct((n_row, own + WROWS, feat), BF16),
        in_specs=[SMEM, SMEM, SMEM, VMEM, VMEM, VMEM],
        out_specs=VMEM,
        scratch_shapes=[
            pltpu.VMEM((row_tiles, size, feat), BF16),
            pltpu.VMEM((col_tiles + 1, size, feat), F32),
        ],
        compiler_params=params(24),
        name="backward",
    )(meta, rows, cols, tiles, mine, other)
    shares = lax.all_to_all(col_partial, "row", 0, 0, tiled=True)
    scale = (own * n_row * peers * 2) ** -0.5

    def finish(parts_ref, grad_ref, chunk_ref):
        final_kernel(parts_ref, grad_ref, chunk_ref, scale)

    input_grad, chunk = pl.pallas_call(
        finish,
        out_shape=[
            jax.ShapeDtypeStruct((own, feat), BF16),
            jax.ShapeDtypeStruct((WROWS, feat), F32),
        ],
        in_specs=[VMEM],
        out_specs=[VMEM, VMEM],
        compiler_params=params(24),
        name="finish",
    )(shares)
    spread_chunk = jnp.broadcast_to(chunk[None], (peers, WROWS, feat))
    whole = lax.all_to_all(spread_chunk, yx, 0, 0, tiled=True).reshape(2, feat, feat)
    weight_grad = jnp.concatenate([whole[0], whole[1]], axis=1)
    return (hidden, input_grad, weight_grad)


def solution(mesh):
    side = 4
    fine = Mesh(
        mesh.devices.reshape(mesh.shape["row"], side, side, 2), ("row", "y", "x", "core")
    )
    col = ("y", "x", "core")
    placed = (
        P((*col, "row"), None),
        P(),
        P("row", col, None, None, None),
        P("row", col, None),
        P("row", col, None),
        P("row", col),
        P(("row", *col), None),
    )
    return jax.shard_map(
        per_device,
        mesh=fine,
        in_specs=placed,
        out_specs=(P(("row", *col), None), P((*col, "row"), None), P()),
        check_vma=False,
    )
```

```python
import jax
import jax.numpy as jnp
from jax import lax
from jax.experimental import pallas as pl
from jax.experimental.pallas import tpu as pltpu
from jax.sharding import Mesh, PartitionSpec as P

F32, BF16, I32 = jnp.float32, jnp.bfloat16, jnp.int32
HIGHEST = lax.Precision.HIGHEST
UNROLL = 16
LIST = 208
CHUNKS = 8
PREPARE = 4
SMEM = pl.BlockSpec(memory_space=pltpu.SMEM)
VMEM = pl.BlockSpec(memory_space=pltpu.VMEM)
HBM = pl.BlockSpec(memory_space=pltpu.HBM)


def params(mebibytes):
    return pltpu.CompilerParams(vmem_limit_bytes=mebibytes * 2**20)


def prepare_kernel(rows, cols, count, words, pairs, open_row, open_col):
    live = count[0, 0]
    core = lax.axis_index("core")
    row_bins, col_bins = open_row.shape[0] - 1, open_col.shape[0] - 1

    for spot in range(row_bins + 1):
        open_row[spot] = -1
    for spot in range(col_bins + 1):
        open_col[spot] = -1

    def step(slot, ends):
        other, mine, first, second = ends
        valid = slot < live
        row, col = rows[0, 0, slot], cols[0, 0, slot]
        own = (((row >> 1) & 1) == core).astype(I32)
        local = ((row >> 2) << 1) + (row & 1)
        spot = jnp.where(valid, row, row_bins)
        waiting = open_row[spot]
        full = jnp.logical_and(waiting >= 0, valid).astype(I32)
        word = waiting + (slot << 9) + (local << 18) + (col << 27)
        words[jnp.where(own == 1, LIST + mine, other)] = word
        open_row[spot] = jnp.where(waiting >= 0, -1, slot + (col << 23))
        place = jnp.where(valid, (col << 1) + own, col_bins)
        paused = open_col[place]
        done = jnp.logical_and(paused >= 0, valid).astype(I32)
        word = paused + (slot << 9) + (col << 18) + (local << 27)
        words[jnp.where(own == 1, 2 * LIST + first, 3 * LIST + second)] = word
        open_col[place] = jnp.where(paused >= 0, -1, slot + (local << 22))
        return (
            other + full * (1 - own),
            mine + full * own,
            first + done * own,
            second + done * (1 - own),
        )

    def several(block, ends):
        for offset in range(PREPARE):
            ends = step(block * PREPARE + offset, ends)
        return ends

    ends = lax.fori_loop(0, pl.cdiv(live, PREPARE), several, (0, 0, 0, 0))

    def flush_row(row, ends):
        other, mine = ends
        own = (((row >> 1) & 1) == core).astype(I32)
        local = ((row >> 2) << 1) + (row & 1)
        waiting = open_row[row]
        full = (waiting >= 0).astype(I32)
        slot, col = waiting & 511, (waiting >> 23) & 15
        words[jnp.where(own == 1, LIST + mine, other)] = (
            waiting + (slot << 9) + (local << 18) + (col << 27)
        )
        return other + full * (1 - own), mine + full * own

    def flush_col(place, ends):
        first, second = ends
        own, col = place & 1, place >> 1
        paused = open_col[place]
        done = (paused >= 0).astype(I32)
        slot, local = paused & 511, (paused >> 22) & 31
        words[jnp.where(own == 1, 2 * LIST + first, 3 * LIST + second)] = (
            paused + (slot << 9) + (col << 18) + (local << 27)
        )
        return first + done * own, second + done * (1 - own)

    other, mine = lax.fori_loop(0, row_bins, flush_row, ends[:2])
    first, second = lax.fori_loop(0, col_bins, flush_col, ends[2:])
    for part, end in enumerate((other, mine, first, second)):
        pairs[part] = end
        for offset in range(UNROLL):
            words[part * LIST + end + offset] = 0


def weight_of(word, spot, total):
    alone = (word & 511) == ((word >> 9) & 511)
    return jnp.where(spot < total, jnp.where(alone, 0.5, 1.0), 0.0)


def start_tiles(live, stored, tiles, sems):
    for chunk in range(sems.shape[0]):
        span = tiles.shape[0] // sems.shape[0]

        @pl.when(chunk * span < live)
        def _():
            tile_copy(chunk, stored, tiles, sems).start()


def tile_copy(chunk, stored, tiles, sems):
    span = tiles.shape[0] // sems.shape[0]
    spot = pl.ds(chunk * span, span)
    return pltpu.make_async_copy(stored.at[0, 0, spot], tiles.at[spot], sems.at[chunk])


def await_tiles(first, last, stored, tiles, sems):
    def body(chunk, carry):
        tile_copy(chunk, stored, tiles, sems).wait()
        return carry

    lax.fori_loop(first, last, body, 0)


def tile_pass(part, words, pairs, tiles, multiply, acc, count=None, stored=None, sems=None):
    total = pairs[part]

    def group(step, loaded):
        listed = [words[part * LIST + step * UNROLL + offset] for offset in range(UNROLL)]
        if stored is not None:
            span = tiles.shape[0] // sems.shape[0]
            needed = loaded
            for word in listed:
                needed = jnp.maximum(needed, ((word >> 9) & 511) // span + 1)
            await_tiles(loaded, needed, stored, tiles, sems)
            loaded = needed
        results = []
        for offset, word in enumerate(listed):
            target, product = multiply(word, tiles)
            weight = weight_of(word, step * UNROLL + offset, total)
            results.append((target, product * weight))
        for target, product in results:
            acc[target] += product
        return loaded

    loaded = lax.fori_loop(0, pl.cdiv(total, UNROLL), group, 0)
    if stored is not None:
        span = tiles.shape[0] // sems.shape[0]
        await_tiles(loaded, pl.cdiv(count[0, 0], span), stored, tiles, sems)


def forward_product(panel):
    def multiply(word, tiles):
        pair = jnp.concatenate([tiles[word & 511], tiles[(word >> 9) & 511]], axis=1)
        source = jnp.concatenate([panel[(word >> 23) & 15], panel[(word >> 27) & 15]], axis=0)
        return (word >> 18) & 31, jnp.dot(pair, source, preferred_element_type=F32)

    return multiply


def backward_product(grads):
    def multiply(word, tiles):
        pair = jnp.concatenate([tiles[word & 511], tiles[(word >> 9) & 511]], axis=0)
        source = jnp.concatenate([grads[(word >> 22) & 31], grads[(word >> 27) & 31]], axis=0)
        product = lax.dot_general(
            pair, source, (((0,), (0,)), ((), ())), preferred_element_type=F32
        )
        return (word >> 18) & 15, product

    return multiply


def forward_send_kernel(words, pairs, count, stored, panel, send, tiles, acc, sems):
    start_tiles(count[0, 0], stored, tiles, sems)
    acc[...] = jnp.zeros_like(acc)
    tile_pass(0, words, pairs, tiles, forward_product(panel), acc, count, stored, sems)
    send[...] = acc[...].astype(BF16)


def forward_keep_kernel(words, pairs, tiles, panel, keep):
    keep[...] = jnp.zeros_like(keep)
    tile_pass(1, words, pairs, tiles, forward_product(panel), keep)


def middle_kernel(parts, weight, cotangent, hidden, payload, local):
    peers = parts.shape[0]
    feat = weight.shape[0]
    agg = parts[0].astype(F32)
    for peer in range(1, peers):
        agg += parts[peer].astype(F32)
    wide = weight[...].astype(F32)
    pre = jnp.dot(agg, wide, precision=HIGHEST, preferred_element_type=F32)
    slope, cubic = 0.7978845608028654, 0.044715
    square = pre * pre
    curve = jnp.tanh(slope * pre * (1.0 + cubic * square))
    cdf = 0.5 * (1.0 + curve)
    hidden[...] = (pre * cdf).astype(BF16)
    rate = cdf + 0.5 * pre * (1.0 - curve * curve) * (slope * (1.0 + 3.0 * cubic * square))
    act = cotangent[...].astype(F32) * rate
    grad = lax.dot_general(
        act.astype(BF16), weight[...], (((1,), (1,)), ((), ())), preferred_element_type=F32
    ).astype(BF16)
    for peer in range(peers):
        payload[peer] = grad
    share = lax.dot_general(
        agg, act, (((0,), (0,)), ((), ())), precision=HIGHEST, preferred_element_type=F32
    ).astype(BF16)
    local[:feat] = share[:, :feat]
    local[feat:] = share[:, feat:]


def backward_first_kernel(words, pairs, count, stored, grads, acc, tiles, sems):
    start_tiles(count[0, 0], stored, tiles, sems)
    acc[...] = jnp.zeros_like(acc)
    tile_pass(2, words, pairs, tiles, backward_product(grads), acc, count, stored, sems)


def backward_second_kernel(words, pairs, tiles, grads, start, out, acc):
    acc[...] = start[...]
    tile_pass(3, words, pairs, tiles, backward_product(grads), acc)
    out[...] = acc[...].astype(BF16)


def finish_kernel(parts, grad):
    total = parts[0].astype(F32)
    for peer in range(1, parts.shape[0]):
        total += parts[peer].astype(F32)
    grad[...] = total.astype(BF16)


def add_kernel(left, right, total):
    total[...] = (left[...].astype(F32) + right[...].astype(F32)).astype(BF16)


def added(*terms):
    terms = [term.astype(F32) for term in terms]
    while len(terms) > 1:
        terms = [left + right for left, right in zip(terms[::2], terms[1::2])]
    return terms[0]


def swapped(value, axis, step):
    return lax.ppermute(value, axis, [(i, i ^ step) for i in range(lax.axis_size(axis))])


def shifted(value, axis, step):
    size = lax.axis_size(axis)
    return lax.ppermute(value, axis, [(i, (i + step) % size) for i in range(size)])


def per_device(features, weight, adj_tiles, tile_rows, tile_cols, tile_count, cotangent):
    own, feat = features.shape
    hid = weight.shape[1]
    n_row = lax.axis_size("row")
    peers = lax.axis_size("y") * lax.axis_size("x")
    slots, size = adj_tiles.shape[2], adj_tiles.shape[-1]
    half_rows = own * peers // size
    col_tiles = own * n_row // size
    yx = ("y", "x")

    stored = pltpu.with_memory_space_constraint(adj_tiles, pltpu.HBM)
    words, pairs = pl.pallas_call(
        prepare_kernel,
        out_shape=[
            jax.ShapeDtypeStruct((4 * LIST,), I32),
            jax.ShapeDtypeStruct((4,), I32),
        ],
        in_specs=[SMEM, SMEM, SMEM],
        out_specs=[SMEM, SMEM],
        scratch_shapes=[
            pltpu.SMEM((2 * half_rows + 1,), I32),
            pltpu.SMEM((2 * col_tiles + 1,), I32),
        ],
        compiler_params=params(4),
        name="prepare",
    )(tile_rows, tile_cols, tile_count)

    spread = jnp.broadcast_to(features[None], (n_row, own, feat))
    panel = lax.all_to_all(spread, "row", 0, 0, tiled=True).reshape(col_tiles, size, feat)
    flops = slots * size * size * feat
    tile_cost = pl.CostEstimate(flops=flops, bytes_accessed=adj_tiles.size, transcendentals=0)
    held = pltpu.VMEM((slots, size, size), BF16)
    sems = pltpu.SemaphoreType.DMA((CHUNKS,))
    send, tiles = pl.pallas_call(
        forward_send_kernel,
        out_shape=[jax.ShapeDtypeStruct((half_rows, size, feat), BF16), held],
        in_specs=[SMEM, SMEM, SMEM, HBM, VMEM],
        out_specs=[VMEM, VMEM],
        scratch_shapes=[pltpu.VMEM((half_rows, size, feat), F32), sems],
        compiler_params=params(16),
        cost_estimate=tile_cost,
        name="forward_send",
    )(words, pairs, tile_count, stored, panel)
    got = swapped(send, "core", 1)
    keep = pl.pallas_call(
        forward_keep_kernel,
        out_shape=jax.ShapeDtypeStruct((half_rows, size, feat), F32),
        in_specs=[SMEM, SMEM, VMEM, VMEM],
        out_specs=VMEM,
        compiler_params=params(16),
        cost_estimate=tile_cost,
        name="forward_keep",
    )(words, pairs, tiles, panel)
    paired = (keep + got.astype(F32)).astype(BF16).reshape(peers, own, feat)
    parts = lax.all_to_all(paired, yx, 0, 0, tiled=True)
    hidden, payload, local = pl.pallas_call(
        middle_kernel,
        out_shape=[
            jax.ShapeDtypeStruct(cotangent.shape, BF16),
            jax.ShapeDtypeStruct((peers, own, feat), BF16),
            jax.ShapeDtypeStruct((hid, feat), BF16),
        ],
        in_specs=[VMEM, VMEM, VMEM],
        out_specs=[VMEM, VMEM, VMEM],
        compiler_params=params(16),
        name="middle",
    )(parts, weight, cotangent)

    step = 1
    while step < n_row:
        local = added(local, swapped(local, "row", step)).astype(BF16)
        step *= 2
    mine = lax.all_to_all(payload, yx, 0, 0, tiled=True).reshape(half_rows, size, feat)
    mine, local = lax.optimization_barrier((mine, local))
    other = swapped(mine, "core", 1)
    paired_local = swapped(local, "core", 1)
    started, tiles = pl.pallas_call(
        backward_first_kernel,
        out_shape=[jax.ShapeDtypeStruct((col_tiles, size, feat), F32), held],
        in_specs=[SMEM, SMEM, SMEM, HBM, VMEM],
        out_specs=[VMEM, VMEM],
        scratch_shapes=[sems],
        compiler_params=params(16),
        cost_estimate=tile_cost,
        name="backward_first",
    )(words, pairs, tile_count, stored, mine)
    col_partial = pl.pallas_call(
        backward_second_kernel,
        out_shape=jax.ShapeDtypeStruct((col_tiles, size, feat), BF16),
        in_specs=[SMEM, SMEM, VMEM, VMEM, VMEM],
        out_specs=VMEM,
        scratch_shapes=[pltpu.VMEM((col_tiles, size, feat), F32)],
        compiler_params=params(16),
        cost_estimate=tile_cost,
        name="backward_second",
    )(words, pairs, tiles, other, started)
    col_partial, local, paired_local = lax.optimization_barrier((col_partial, local, paired_local))
    local = pl.pallas_call(
        add_kernel,
        out_shape=jax.ShapeDtypeStruct(local.shape, BF16),
        in_specs=[VMEM, VMEM],
        out_specs=VMEM,
        compiler_params=params(4),
        cost_estimate=tile_cost,
        name="add_core",
    )(local, paired_local)
    shares = lax.all_to_all(col_partial.reshape(n_row, own, feat), "row", 0, 0, tiled=True)
    local = added(local, *[shifted(local, "x", step) for step in (2, 1, 3)]).astype(BF16)
    total = added(local, *[shifted(local, "y", step) for step in (2, 1, 3)])
    total = total * (own * n_row * peers * 2) ** -0.5
    weight_grad = jnp.concatenate([total[:feat], total[feat:]], axis=1)
    input_grad = pl.pallas_call(
        finish_kernel,
        out_shape=jax.ShapeDtypeStruct((own, feat), BF16),
        in_specs=[VMEM],
        out_specs=VMEM,
        compiler_params=params(16),
        name="finish",
    )(shares)
    return (hidden, input_grad, weight_grad)


def solution(mesh):
    side = 4
    fine = Mesh(
        mesh.devices.reshape(mesh.shape["row"], side, side, 2), ("row", "y", "x", "core")
    )
    col = ("y", "x", "core")
    placed = (
        P((*col, "row"), None),
        P(),
        P("row", col, None, None, None),
        P("row", col, None),
        P("row", col, None),
        P("row", col),
        P(("row", *col), None),
    )
    return jax.shard_map(
        per_device,
        mesh=fine,
        in_specs=placed,
        out_specs=(P(("row", *col), None), P((*col, "row"), None), P()),
        check_vma=False,
    )
```

```python
import jax
import jax.numpy as jnp
from jax import lax
from jax.experimental import pallas as pl
from jax.experimental.pallas import tpu as pltpu
from jax.sharding import Mesh, PartitionSpec as P

F32, BF16, I32 = jnp.float32, jnp.bfloat16, jnp.int32
HIGHEST = lax.Precision.HIGHEST
UNROLL = 16
LIST = 208
CHUNKS = 8
AHEAD = 8
PREPARE = 4
SMEM = pl.BlockSpec(memory_space=pltpu.SMEM)
VMEM = pl.BlockSpec(memory_space=pltpu.VMEM)
HBM = pl.BlockSpec(memory_space=pltpu.HBM)


def params(mebibytes):
    return pltpu.CompilerParams(vmem_limit_bytes=mebibytes * 2**20)


def prepare_kernel(forward, rows, cols, count, *refs):
    if forward:
        stored, words, pairs, tiles, waiting, sem = refs
        load = pltpu.make_async_copy(stored.at[0, 0], tiles, sem)
        load.start()
    else:
        words, pairs, waiting = refs
    live = count[0, 0]
    core = lax.axis_index("core")
    bins = waiting.shape[0] - 1
    target_at, source_at, partner_at = (18, 23, 27) if forward else (18, 22, 27)

    for spot in range(bins + 1):
        waiting[spot] = -1

    def enter(ends, here, open_word, closing, valid):
        first, second = ends
        full = jnp.logical_and(open_word >= 0, valid).astype(I32)
        words[jnp.where(here == 1, LIST + second, first)] = open_word + closing
        return first + full * (1 - here), second + full * here

    def step(slot, ends):
        valid = slot < live
        row, col = rows[0, 0, slot], cols[0, 0, slot]
        own = (((row >> 1) & 1) == core).astype(I32)
        local = ((row >> 2) << 1) + (row & 1)
        if forward:
            place, target, source, here = row, local, col, own
        else:
            place, target, source, here = (col << 1) + own, col, local, 1 - own
        place = jnp.where(valid, place, bins)
        held = waiting[place]
        waiting[place] = jnp.where(held >= 0, -1, slot + (source << source_at))
        closing = (slot << 9) + (target << target_at) + (source << partner_at)
        return enter(ends, here, held, closing, valid)

    def several(block, ends):
        for offset in range(PREPARE):
            ends = step(block * PREPARE + offset, ends)
        return ends

    def flush(block, ends):
        for offset in range(PREPARE):
            place = block * PREPARE + offset
            held = waiting[place]
            if forward:
                here = (((place >> 1) & 1) == core).astype(I32)
                target = ((place >> 2) << 1) + (place & 1)
                source = (held >> source_at) & 15
            else:
                here, target = 1 - (place & 1), place >> 1
                source = (held >> source_at) & 31
            closing = ((held & 511) << 9) + (target << target_at) + (source << partner_at)
            ends = enter(ends, here, held, closing, True)
        return ends

    ends = lax.fori_loop(0, pl.cdiv(live, PREPARE), several, (0, 0))
    ends = lax.fori_loop(0, bins // PREPARE, flush, ends)
    for part, end in enumerate(ends):
        pairs[part] = end
        for offset in range(UNROLL):
            words[part * LIST + end + offset] = 0
    if forward:
        load.wait()


def weight_of(word, spot, total):
    alone = (word & 511) == ((word >> 9) & 511)
    return jnp.where(spot < total, jnp.where(alone, 0.5, 1.0), 0.0)


def tile_copy(chunk, stored, tiles, sems):
    span = tiles.shape[0] // CHUNKS
    spot = pl.ds(chunk * span, span)
    return pltpu.make_async_copy(stored.at[0, 0, spot], tiles.at[spot], sems.at[chunk])


def start_tiles(chunk, live, stored, tiles, sems):
    span = tiles.shape[0] // CHUNKS

    @pl.when(chunk * span < live)
    def _():
        tile_copy(chunk, stored, tiles, sems).start()


def await_tiles(first, last, live, stored, tiles, sems):
    def body(chunk, carry):
        tile_copy(chunk, stored, tiles, sems).wait()
        start_tiles(chunk + AHEAD, live, stored, tiles, sems)
        return carry

    lax.fori_loop(first, last, body, 0)


def tile_pass(part, words, pairs, tiles, multiply, acc, count=None, stored=None, sems=None):
    total = pairs[part]

    def group(step, loaded):
        listed = [words[part * LIST + step * UNROLL + offset] for offset in range(UNROLL)]
        if stored is not None:
            span = tiles.shape[0] // CHUNKS
            highest = 0
            for word in listed:
                highest = jnp.maximum(highest, (word >> 9) & 511)
            needed = jnp.maximum(loaded, highest // span + 1)
            await_tiles(loaded, needed, count[0, 0], stored, tiles, sems)
            loaded = needed
        results = []
        for offset, word in enumerate(listed):
            target, product = multiply(word, tiles)
            weight = weight_of(word, step * UNROLL + offset, total)
            results.append((target, product * weight))
        for target, product in results:
            acc[target] += product
        return loaded

    loaded = lax.fori_loop(0, pl.cdiv(total, UNROLL), group, 0)
    if stored is not None:
        span = tiles.shape[0] // CHUNKS
        await_tiles(loaded, pl.cdiv(count[0, 0], span), count[0, 0], stored, tiles, sems)


def forward_product(panel):
    def multiply(word, tiles):
        pair = jnp.concatenate([tiles[word & 511], tiles[(word >> 9) & 511]], axis=1)
        source = jnp.concatenate([panel[(word >> 23) & 15], panel[(word >> 27) & 15]], axis=0)
        return (word >> 18) & 31, jnp.dot(pair, source, preferred_element_type=F32)

    return multiply


def backward_product(grads):
    def multiply(word, tiles):
        pair = jnp.concatenate([tiles[word & 511], tiles[(word >> 9) & 511]], axis=0)
        source = jnp.concatenate([grads[(word >> 22) & 31], grads[(word >> 27) & 31]], axis=0)
        product = lax.dot_general(
            pair, source, (((0,), (0,)), ((), ())), preferred_element_type=F32
        )
        return (word >> 18) & 15, product

    return multiply


def forward_send_kernel(words, pairs, tiles, *refs):
    *blocks, send, panel, acc = refs
    here = lax.axis_index("row")
    per_block = panel.shape[0] // len(blocks)
    for step, block in enumerate(blocks):
        owner = lax.rem(here - step + len(blocks), len(blocks))
        for part in range(per_block):
            spot = pl.ds(part * panel.shape[1], panel.shape[1])
            panel[owner * per_block + part] = block[spot]
    acc[...] = jnp.zeros_like(acc)
    tile_pass(0, words, pairs, tiles, forward_product(panel), acc)
    send[...] = acc[...].astype(BF16)


def forward_keep_kernel(words, pairs, tiles, panel, keep):
    keep[...] = jnp.zeros_like(keep)
    tile_pass(1, words, pairs, tiles, forward_product(panel), keep)


def middle_kernel(parts, weight, cotangent, hidden, payload, local):
    peers = parts.shape[0]
    feat = weight.shape[0]
    agg = parts[0].astype(F32)
    for peer in range(1, peers):
        agg += parts[peer].astype(F32)
    wide = weight[...].astype(F32)
    pre = jnp.dot(agg, wide, precision=HIGHEST, preferred_element_type=F32)
    slope, cubic = 0.7978845608028654, 0.044715
    square = pre * pre
    curve = jnp.tanh(slope * pre * (1.0 + cubic * square))
    cdf = 0.5 * (1.0 + curve)
    hidden[...] = (pre * cdf).astype(BF16)
    rate = cdf + 0.5 * pre * (1.0 - curve * curve) * (slope * (1.0 + 3.0 * cubic * square))
    act = cotangent[...].astype(F32) * rate
    grad = lax.dot_general(
        act.astype(BF16), weight[...], (((1,), (1,)), ((), ())), preferred_element_type=F32
    ).astype(BF16)
    for peer in range(peers):
        payload[peer] = grad
    share = lax.dot_general(
        agg, act, (((0,), (0,)), ((), ())), precision=HIGHEST, preferred_element_type=F32
    ).astype(BF16)
    local[:feat] = share[:, :feat]
    local[feat:] = share[:, feat:]


def backward_first_kernel(words, pairs, count, stored, grads, acc, tiles, sems):
    for chunk in range(AHEAD):
        start_tiles(chunk, count[0, 0], stored, tiles, sems)
    acc[...] = jnp.zeros_like(acc)
    tile_pass(0, words, pairs, tiles, backward_product(grads), acc, count, stored, sems)


def backward_second_kernel(words, pairs, tiles, grads, start, out, acc):
    acc[...] = start[...]
    tile_pass(1, words, pairs, tiles, backward_product(grads), acc)
    per_peer = out.shape[1] // acc.shape[1]
    for peer in range(out.shape[0]):
        for part in range(per_peer):
            spot = pl.ds(part * acc.shape[1], acc.shape[1])
            out[peer, spot] = acc[peer * per_peer + part].astype(BF16)


def finish_kernel(scale, parts, first, second, third, fourth, grad, weight_grad):
    total = parts[0].astype(F32)
    for peer in range(1, parts.shape[0]):
        total += parts[peer].astype(F32)
    grad[...] = total.astype(BF16)
    feat = grad.shape[1]
    total = added(first[...], second[...], third[...], fourth[...]) * scale
    weight_grad[:, :feat] = total[:feat]
    weight_grad[:, feat:] = total[feat:]


def add_kernel(*refs):
    *terms, total = refs
    total[...] = added(*[term[...] for term in terms]).astype(BF16)


def summed(*terms):
    return pl.pallas_call(
        add_kernel,
        out_shape=jax.ShapeDtypeStruct(terms[0].shape, BF16),
        in_specs=[VMEM] * len(terms),
        out_specs=VMEM,
        compiler_params=params(4),
        name="add",
    )(*terms)


def added(*terms):
    terms = [term.astype(F32) for term in terms]
    while len(terms) > 1:
        terms = [left + right for left, right in zip(terms[::2], terms[1::2])]
    return terms[0]


def swapped(value, axis, step):
    return lax.ppermute(value, axis, [(i, i ^ step) for i in range(lax.axis_size(axis))])


def shifted(value, axis, step):
    size = lax.axis_size(axis)
    return lax.ppermute(value, axis, [(i, (i + step) % size) for i in range(size)])


def per_device(features, weight, adj_tiles, tile_rows, tile_cols, tile_count, cotangent):
    own, feat = features.shape
    hid = weight.shape[1]
    n_row = lax.axis_size("row")
    peers = lax.axis_size("y") * lax.axis_size("x")
    slots, size = adj_tiles.shape[2], adj_tiles.shape[-1]
    half_rows = own * peers // size
    col_tiles = own * n_row // size
    yx = ("y", "x")

    stored = pltpu.with_memory_space_constraint(adj_tiles, pltpu.HBM)
    rows, cols = [pltpu.with_memory_space_constraint(v, pltpu.HBM) for v in (tile_rows, tile_cols)]
    places = (rows, cols, tile_count)
    held = pltpu.VMEM((slots, size, size), BF16)
    lists = [jax.ShapeDtypeStruct((2 * LIST,), I32), jax.ShapeDtypeStruct((2,), I32)]

    def prepare(forward, bins, operands):
        def kernel(*refs):
            prepare_kernel(forward, *refs)

        sem = pltpu.SemaphoreType.DMA(())
        return pl.pallas_call(
            kernel,
            out_shape=[*lists, *([held] if forward else [])],
            in_specs=[SMEM, SMEM, SMEM, *([HBM] if forward else [])],
            out_specs=[SMEM, SMEM, *([VMEM] if forward else [])],
            scratch_shapes=[pltpu.SMEM((bins + 1,), I32), *([sem] if forward else [])],
            compiler_params=params(4),
            name="prepare_forward" if forward else "prepare_backward",
        )(*operands)

    arrived = {way: shifted(features, "row", way) for way in (4, 3, 5, 2, 6, 1, 7)}
    words, pairs, resident = prepare(True, 2 * half_rows, (*places, stored))
    flops = slots * size * size * feat
    tile_cost = pl.CostEstimate(flops=flops, bytes_accessed=adj_tiles.size, transcendentals=0)
    send, panel = pl.pallas_call(
        forward_send_kernel,
        out_shape=[
            jax.ShapeDtypeStruct((half_rows, size, feat), BF16),
            jax.ShapeDtypeStruct((col_tiles, size, feat), BF16),
        ],
        in_specs=[SMEM, SMEM, VMEM, *([VMEM] * n_row)],
        out_specs=[VMEM, VMEM],
        scratch_shapes=[pltpu.VMEM((half_rows, size, feat), F32)],
        compiler_params=params(16),
        cost_estimate=tile_cost,
        name="forward_send",
    )(words, pairs, resident, features, *[arrived[way] for way in range(1, n_row)])
    got = swapped(send, "core", 1)
    keep = pl.pallas_call(
        forward_keep_kernel,
        out_shape=jax.ShapeDtypeStruct((half_rows, size, feat), F32),
        in_specs=[SMEM, SMEM, VMEM, VMEM],
        out_specs=VMEM,
        compiler_params=params(16),
        cost_estimate=tile_cost,
        name="forward_keep",
    )(words, pairs, resident, panel)
    paired = (keep + got.astype(F32)).astype(BF16).reshape(peers, own, feat)
    paired, words, pairs = lax.optimization_barrier((paired, words, pairs))
    words, pairs = prepare(False, 2 * col_tiles, (rows, cols, tile_count + 0 * pairs[:1, None]))
    parts = lax.all_to_all(paired, yx, 0, 0, tiled=True)
    parts, words, pairs = lax.optimization_barrier((parts, words, pairs))
    hidden, payload, local = pl.pallas_call(
        middle_kernel,
        out_shape=[
            jax.ShapeDtypeStruct(cotangent.shape, BF16),
            jax.ShapeDtypeStruct((peers, own, feat), BF16),
            jax.ShapeDtypeStruct((hid, feat), BF16),
        ],
        in_specs=[VMEM, VMEM, VMEM],
        out_specs=[VMEM, VMEM, VMEM],
        compiler_params=params(16),
        name="middle",
    )(parts, weight, cotangent)

    local = added(local, swapped(local, "row", 1)).astype(BF16)
    local = added(local, *[shifted(local, "row", step) for step in (4, 2, 6)]).astype(BF16)
    mine = lax.all_to_all(payload, yx, 0, 0, tiled=True).reshape(half_rows, size, feat)
    mine, local = lax.optimization_barrier((mine, local))
    other = swapped(mine, "core", 1)
    paired_local = swapped(local, "core", 1)
    started, tiles = pl.pallas_call(
        backward_first_kernel,
        out_shape=[jax.ShapeDtypeStruct((col_tiles, size, feat), F32), held],
        in_specs=[SMEM, SMEM, SMEM, HBM, VMEM],
        out_specs=[VMEM, VMEM],
        scratch_shapes=[pltpu.SemaphoreType.DMA((CHUNKS,))],
        compiler_params=params(16),
        cost_estimate=tile_cost,
        name="backward_first",
    )(words, pairs, tile_count, stored, mine)
    col_partial = pl.pallas_call(
        backward_second_kernel,
        out_shape=jax.ShapeDtypeStruct((n_row, own, feat), BF16),
        in_specs=[SMEM, SMEM, VMEM, VMEM, VMEM],
        out_specs=VMEM,
        scratch_shapes=[pltpu.VMEM((col_tiles, size, feat), F32)],
        compiler_params=params(16),
        cost_estimate=tile_cost,
        name="backward_second",
    )(words, pairs, tiles, other, started)
    col_partial, local, paired_local = lax.optimization_barrier((col_partial, local, paired_local))
    shares = lax.all_to_all(col_partial, "row", 0, 0, tiled=True)
    local = summed(local, paired_local)
    local = summed(local, *[shifted(local, "x", step) for step in (2, 1, 3)])
    last = [local, *[shifted(local, "y", step) for step in (2, 1, 3)]]
    scale = (own * n_row * peers * 2) ** -0.5

    def finish(*refs):
        finish_kernel(scale, *refs)

    input_grad, weight_grad = pl.pallas_call(
        finish,
        out_shape=[
            jax.ShapeDtypeStruct((own, feat), BF16),
            jax.ShapeDtypeStruct((feat, hid), F32),
        ],
        in_specs=[VMEM] * 5,
        out_specs=[VMEM, VMEM],
        compiler_params=params(16),
        name="finish",
    )(shares, *last)
    return (hidden, input_grad, weight_grad)


def solution(mesh):
    side = 4
    fine = Mesh(
        mesh.devices.reshape(mesh.shape["row"], side, side, 2), ("row", "y", "x", "core")
    )
    col = ("y", "x", "core")
    placed = (
        P((*col, "row"), None),
        P(),
        P("row", col, None, None, None),
        P("row", col, None),
        P("row", col, None),
        P("row", col),
        P(("row", *col), None),
    )
    return jax.shard_map(
        per_device,
        mesh=fine,
        in_specs=placed,
        out_specs=(P(("row", *col), None), P((*col, "row"), None), P()),
        check_vma=False,
    )
```

```python
import jax
import jax.numpy as jnp
from jax import lax
from jax.experimental import pallas as pl
from jax.experimental.pallas import tpu as pltpu
from jax.sharding import Mesh, PartitionSpec as P

F32, BF16, I32 = jnp.float32, jnp.bfloat16, jnp.int32
HIGHEST = lax.Precision.HIGHEST
UNROLL = 16
LIST = 240
WORDS = 512
CHUNKS = 8
AHEAD = 8
NEAR = (1, 7, 2, 6, 3, 5)
SMEM = pl.BlockSpec(memory_space=pltpu.SMEM)
VMEM = pl.BlockSpec(memory_space=pltpu.VMEM)
HBM = pl.BlockSpec(memory_space=pltpu.HBM)


def params(mebibytes):
    return pltpu.CompilerParams(vmem_limit_bytes=mebibytes * 2**20)


def stacked(shape, *rows):
    spot = lax.broadcasted_iota(I32, shape, 0)
    out = jnp.zeros(shape, F32)
    for index, row in enumerate(rows):
        out = jnp.where(spot == index, row.astype(F32), out)
    return out.astype(BF16)


def ones_where(mask):
    return jnp.where(mask, 1.0, 0.0).astype(BF16)


def over_lanes(left, right):
    return lax.dot_general(left, right, (((1,), (1,)), ((), ())), preferred_element_type=F32)


def write_list(key, own, bins, part_of_bin, target, source, source_at, slot, valid, earlier, words):
    slots, width = slot.shape[1], words.shape[1]
    member = jnp.logical_and(lax.broadcasted_iota(I32, (bins, slots), 0) == key, valid)
    before = jnp.dot(
        ones_where(member), earlier[:slots, :slots], preferred_element_type=F32
    )
    rank = jnp.sum(jnp.where(member, before, 0.0), axis=0, keepdims=True).astype(I32)
    name = jnp.where(valid, (rank >> 1) * bins + key, -1)
    named = lax.broadcasted_iota(I32, (width, slots), 0) == name
    closes = (rank & 1) == 1
    closing = [jnp.logical_and(jnp.logical_and(closes, valid), own == index) for index in range(2)]
    marks = stacked((8, slots), *[jnp.where(mask, 1.0, 0.0) for mask in closing])
    ahead = jnp.dot(marks, earlier[:slots, :slots], preferred_element_type=F32)
    turn = jnp.where(own == 1, ahead[1:2], ahead[0:1])
    fields = stacked(
        (8, slots), slot >> 1, slot & 1, source, target, jnp.ones_like(slot), turn
    )
    opened = over_lanes(fields, ones_where(jnp.logical_and(named, jnp.logical_not(closes))))
    closed = over_lanes(fields, ones_where(jnp.logical_and(named, closes)))
    lane = lax.broadcasted_iota(I32, (1, width), 1)
    part = part_of_bin(lane & (bins - 1))
    used, paired = opened[4:5] > 0.5, closed[4:5] > 0.5
    masks = [jnp.logical_and(used, part == index) for index in range(2)]
    singles = [jnp.logical_and(mask, jnp.logical_not(paired)) for mask in masks]
    marks = stacked((8, width), *[jnp.where(mask, 1.0, 0.0) for mask in singles])
    ahead = jnp.dot(marks, earlier, preferred_element_type=F32)
    place = jnp.full((1, width), -1, I32)
    for index, (mask, single) in enumerate(zip(masks, singles)):
        couples = jnp.where(jnp.logical_and(mask, paired), 1.0, 0.0)
        alone = jnp.sum(couples, axis=1, keepdims=True) + ahead[index : index + 1]
        spot = jnp.where(single, alone, closed[5:6]).astype(I32) + index * LIST
        place = jnp.where(mask, spot, place)
    other = [jnp.where(paired, closed[index : index + 1], opened[index : index + 1]) for index in range(3)]
    fields = stacked((8, width), *[opened[index : index + 1] for index in range(4)], *other)
    moved = over_lanes(
        fields, ones_where(lax.broadcasted_iota(I32, (width, width), 0) == place)
    ).astype(I32)
    high, low, source_a, target, high_b, low_b, source_b = [moved[k : k + 1] for k in range(7)]
    word = 2 * high + low + ((2 * high_b + low_b) << 9)
    word = word + (target << 18) + (source_a << source_at) + (source_b << 27)
    for index, mask in enumerate(masks):
        length = jnp.sum(jnp.where(mask, 1.0, 0.0), axis=1, keepdims=True).astype(I32)
        word = jnp.where(lane == width - 2 + index, length, word)
    words[...] = word


def prepare_kernel(rows, cols, count, forward_words, backward_words, padded):
    core = lax.axis_index("core")
    padded[...] = jnp.zeros_like(padded)
    padded[0:1, : rows.shape[2]] = rows[0]
    padded[1:2, : rows.shape[2]] = cols[0]
    row, col = padded[0:1], padded[1:2]
    slot = lax.broadcasted_iota(I32, row.shape, 1)
    valid = slot < count[0, 0]
    width = forward_words.shape[1]
    earlier = ones_where(
        lax.broadcasted_iota(I32, (width, width), 0) < lax.broadcasted_iota(I32, (width, width), 1)
    )
    own = jnp.where(((row >> 1) & 1) == core, 1, 0)
    local = ((row >> 2) << 1) + (row & 1)
    shared = (slot, valid, earlier)

    def forward_part(row):
        return jnp.where(((row >> 1) & 1) == core, 1, 0)

    def backward_part(place):
        return 1 - (place & 1)

    write_list(row, own, 64, forward_part, local, col, 23, *shared, forward_words)
    write_list((col << 1) + own, 1 - own, 32, backward_part, col, local, 22, *shared, backward_words)


def weight_of(word, spot, total):
    alone = (word & 511) == ((word >> 9) & 511)
    return jnp.where(spot < total, jnp.where(alone, 0.5, 1.0), 0.0)


def tile_copy(chunk, stored, tiles, sems):
    span = tiles.shape[0] // CHUNKS
    spot = pl.ds(chunk * span, span)
    return pltpu.make_async_copy(stored.at[0, 0, spot], tiles.at[spot], sems.at[chunk])


def start_tiles(chunk, live, stored, tiles, sems):
    span = tiles.shape[0] // CHUNKS

    @pl.when(chunk * span < live)
    def _():
        tile_copy(chunk, stored, tiles, sems).start()


def await_tiles(first, last, live, stored, tiles, sems):
    def body(chunk, carry):
        tile_copy(chunk, stored, tiles, sems).wait()
        start_tiles(chunk + AHEAD, live, stored, tiles, sems)
        return carry

    lax.fori_loop(first, last, body, 0)


def tile_pass(part, words, tiles, multiply, acc, count=None, stored=None, sems=None):
    total = words[0, words.shape[1] - 2 + part]

    def group(step, loaded):
        listed = [words[0, part * LIST + step * UNROLL + offset] for offset in range(UNROLL)]
        if stored is not None:
            span = tiles.shape[0] // CHUNKS
            highest = 0
            for word in listed:
                highest = jnp.maximum(highest, (word >> 9) & 511)
            needed = jnp.maximum(loaded, highest // span + 1)
            await_tiles(loaded, needed, count[0, 0], stored, tiles, sems)
            loaded = needed
        results = []
        for offset, word in enumerate(listed):
            target, product = multiply(word, tiles)
            weight = weight_of(word, step * UNROLL + offset, total)
            results.append((target, product * weight))
        for target, product in results:
            acc[target] += product
        return loaded

    loaded = lax.fori_loop(0, pl.cdiv(total, UNROLL), group, 0)
    if stored is not None:
        span = tiles.shape[0] // CHUNKS
        await_tiles(loaded, pl.cdiv(count[0, 0], span), count[0, 0], stored, tiles, sems)


def forward_product(panel):
    def multiply(word, tiles):
        pair = jnp.concatenate([tiles[word & 511], tiles[(word >> 9) & 511]], axis=1)
        source = jnp.concatenate([panel[(word >> 23) & 15], panel[(word >> 27) & 15]], axis=0)
        return (word >> 18) & 31, jnp.dot(pair, source, preferred_element_type=F32)

    return multiply


def backward_product(grads):
    def multiply(word, tiles):
        pair = jnp.concatenate([tiles[word & 511], tiles[(word >> 9) & 511]], axis=0)
        source = jnp.concatenate([grads[(word >> 22) & 31], grads[(word >> 27) & 31]], axis=0)
        product = lax.dot_general(
            pair, source, (((0,), (0,)), ((), ())), preferred_element_type=F32
        )
        return (word >> 18) & 15, product

    return multiply


def forward_send_kernel(words, tiles, *refs):
    *blocks, low, high, send, panel, acc = refs
    here, rows = lax.axis_index("row"), lax.axis_size("row")
    size = panel.shape[1]
    for distance, block in zip((0, *NEAR), blocks):
        owner = lax.rem(here - distance + rows, rows)
        for part in range(block.shape[0] // size):
            panel[2 * owner + part] = block[pl.ds(part * size, size)]
    opposite = lax.rem(here + rows // 2, rows)
    panel[2 * opposite] = low[...]
    panel[2 * opposite + 1] = high[...]
    acc[...] = jnp.zeros_like(acc)
    tile_pass(0, words, tiles, forward_product(panel), acc)
    send[...] = acc[...].astype(BF16)


def forward_keep_kernel(words, tiles, panel, keep):
    keep[...] = jnp.zeros_like(keep)
    tile_pass(1, words, tiles, forward_product(panel), keep)


def middle_kernel(parts, weight, cotangent, hidden, payload, keep, send):
    peers = parts.shape[0]
    feat = weight.shape[0]
    agg = parts[0].astype(F32)
    for peer in range(1, peers):
        agg += parts[peer].astype(F32)
    wide = weight[...].astype(F32)
    pre = jnp.dot(agg, wide, precision=HIGHEST, preferred_element_type=F32)
    slope, cubic = 0.7978845608028654, 0.044715
    square = pre * pre
    curve = jnp.tanh(slope * pre * (1.0 + cubic * square))
    cdf = 0.5 * (1.0 + curve)
    hidden[...] = (pre * cdf).astype(BF16)
    rate = cdf + 0.5 * pre * (1.0 - curve * curve) * (slope * (1.0 + 3.0 * cubic * square))
    act = cotangent[...].astype(F32) * rate
    grad = lax.dot_general(
        act.astype(BF16), weight[...], (((1,), (1,)), ((), ())), preferred_element_type=F32
    ).astype(BF16)
    for peer in range(peers):
        payload[peer] = grad
    share = lax.dot_general(
        agg, act, (((0,), (0,)), ((), ())), precision=HIGHEST, preferred_element_type=F32
    ).astype(BF16)
    first = lax.axis_index("core") == 0
    keep[...] = jnp.where(first, share[:, :feat], share[:, feat:])
    send[...] = jnp.where(first, share[:, feat:], share[:, :feat])


def backward_first_kernel(words, count, stored, grads, acc, tiles, sems):
    for chunk in range(AHEAD):
        start_tiles(chunk, count[0, 0], stored, tiles, sems)
    acc[...] = jnp.zeros_like(acc)
    tile_pass(0, words, tiles, backward_product(grads), acc, count, stored, sems)


def backward_second_kernel(words, tiles, grads, start, out, acc):
    acc[...] = start[...]
    tile_pass(1, words, tiles, backward_product(grads), acc)
    per_peer = out.shape[1] // acc.shape[1]
    for peer in range(out.shape[0]):
        for part in range(per_peer):
            spot = pl.ds(part * acc.shape[1], acc.shape[1])
            out[peer, spot] = acc[peer * per_peer + part].astype(BF16)


def finish_kernel(scale, parts, mine, other, grad, weight_grad):
    total = parts[0].astype(F32)
    for peer in range(1, parts.shape[0]):
        total += parts[peer].astype(F32)
    grad[...] = total.astype(BF16)
    feat = grad.shape[1]
    left = lax.axis_index("core") == 0
    weight_grad[:, :feat] = jnp.where(left, mine[...], other[...]).astype(F32) * scale
    weight_grad[:, feat:] = jnp.where(left, other[...], mine[...]).astype(F32) * scale


def add_kernel(*refs):
    *terms, total = refs
    total[...] = added(*[term[...] for term in terms]).astype(BF16)


def summed(*terms):
    return pl.pallas_call(
        add_kernel,
        out_shape=jax.ShapeDtypeStruct(terms[0].shape, BF16),
        in_specs=[VMEM] * len(terms),
        out_specs=VMEM,
        compiler_params=params(4),
        name="add",
    )(*terms)


def added(*terms):
    terms = [term.astype(F32) for term in terms]
    while len(terms) > 1:
        terms = [left + right for left, right in zip(terms[::2], terms[1::2])]
    return terms[0]


def swapped(value, axis, step):
    return lax.ppermute(value, axis, [(i, i ^ step) for i in range(lax.axis_size(axis))])


def shifted(value, axis, step):
    size = lax.axis_size(axis)
    return lax.ppermute(value, axis, [(i, (i + step) % size) for i in range(size)])


def per_device(features, weight, adj_tiles, tile_rows, tile_cols, tile_count, cotangent):
    own, feat = features.shape
    hid = weight.shape[1]
    n_row = lax.axis_size("row")
    peers = lax.axis_size("y") * lax.axis_size("x")
    slots, size = adj_tiles.shape[2], adj_tiles.shape[-1]
    half_rows = own * peers // size
    col_tiles = own * n_row // size
    yx = ("y", "x")

    stored = pltpu.with_memory_space_constraint(adj_tiles, pltpu.HBM)
    held = pltpu.VMEM((slots, size, size), BF16)
    list_shape = jax.ShapeDtypeStruct((1, WORDS), I32)
    forward_words, backward_words = pl.pallas_call(
        prepare_kernel,
        out_shape=[list_shape, list_shape],
        in_specs=[VMEM, VMEM, SMEM],
        out_specs=[VMEM, VMEM],
        scratch_shapes=[pltpu.VMEM((8, -(-slots // 128) * 128), I32)],
        compiler_params=params(16),
        cost_estimate=pl.CostEstimate(flops=10**10, bytes_accessed=0, transcendentals=0),
        name="prepare",
    )(
        *[pltpu.with_memory_space_constraint(v, pltpu.HBM) for v in (tile_rows, tile_cols)],
        tile_count,
    )
    resident = pltpu.with_memory_space_constraint(
        adj_tiles.reshape(slots, size, size), pltpu.VMEM
    )
    after, before, after2, before2 = [shifted(features, "row", way) for way in NEAR[:4]]
    after3, before3 = shifted(after2, "row", 1), shifted(before2, "row", 7)
    low, high = shifted(after2[:size], "row", 2), shifted(before2[size:], "row", 6)
    blocks = (features, after, before, after2, before2, after3, before3)
    flops = slots * size * size * feat
    tile_cost = pl.CostEstimate(flops=flops, bytes_accessed=adj_tiles.size, transcendentals=0)
    send, panel = pl.pallas_call(
        forward_send_kernel,
        out_shape=[
            jax.ShapeDtypeStruct((half_rows, size, feat), BF16),
            jax.ShapeDtypeStruct((col_tiles, size, feat), BF16),
        ],
        in_specs=[SMEM, VMEM, *([VMEM] * (n_row + 1))],
        out_specs=[VMEM, VMEM],
        scratch_shapes=[pltpu.VMEM((half_rows, size, feat), F32)],
        compiler_params=params(16),
        cost_estimate=tile_cost,
        name="forward_send",
    )(forward_words, resident, *blocks, low, high)
    got = swapped(send, "core", 1)
    keep = pl.pallas_call(
        forward_keep_kernel,
        out_shape=jax.ShapeDtypeStruct((half_rows, size, feat), F32),
        in_specs=[SMEM, VMEM, VMEM],
        out_specs=VMEM,
        compiler_params=params(16),
        cost_estimate=tile_cost,
        name="forward_keep",
    )(forward_words, resident, panel)
    paired = (keep + got.astype(F32)).astype(BF16).reshape(peers, own, feat)
    parts = lax.all_to_all(paired, yx, 0, 0, tiled=True)
    hidden, payload, local, given = pl.pallas_call(
        middle_kernel,
        out_shape=[
            jax.ShapeDtypeStruct(cotangent.shape, BF16),
            jax.ShapeDtypeStruct((peers, own, feat), BF16),
            jax.ShapeDtypeStruct((feat, hid // 2), BF16),
            jax.ShapeDtypeStruct((feat, hid // 2), BF16),
        ],
        in_specs=[VMEM, VMEM, VMEM],
        out_specs=[VMEM, VMEM, VMEM, VMEM],
        compiler_params=params(16),
        name="middle",
    )(parts, weight, cotangent)

    local = added(local, swapped(given, "core", 1)).astype(BF16)
    local = added(local, swapped(local, "row", 1)).astype(BF16)
    local = added(local, *[shifted(local, "row", step) for step in (4, 2, 6)]).astype(BF16)
    mine = lax.all_to_all(payload, yx, 0, 0, tiled=True).reshape(half_rows, size, feat)
    mine, local = lax.optimization_barrier((mine, local))
    other = swapped(mine, "core", 1)
    beside = swapped(local, "x", 1)
    started, tiles = pl.pallas_call(
        backward_first_kernel,
        out_shape=[jax.ShapeDtypeStruct((col_tiles, size, feat), F32), held],
        in_specs=[SMEM, SMEM, HBM, VMEM],
        out_specs=[VMEM, VMEM],
        scratch_shapes=[pltpu.SemaphoreType.DMA((CHUNKS,))],
        compiler_params=params(16),
        cost_estimate=tile_cost,
        name="backward_first",
    )(backward_words, tile_count, stored, mine)
    col_partial = pl.pallas_call(
        backward_second_kernel,
        out_shape=jax.ShapeDtypeStruct((n_row, own, feat), BF16),
        in_specs=[SMEM, VMEM, VMEM, VMEM],
        out_specs=VMEM,
        scratch_shapes=[pltpu.VMEM((col_tiles, size, feat), F32)],
        compiler_params=params(16),
        cost_estimate=tile_cost,
        name="backward_second",
    )(backward_words, tiles, other, started)
    col_partial, local, beside = lax.optimization_barrier((col_partial, local, beside))
    shares = lax.all_to_all(col_partial, "row", 0, 0, tiled=True)
    local = summed(local, beside)
    local = summed(local, swapped(local, "x", 2))
    local = summed(local, *[shifted(local, "y", step) for step in (2, 1, 3)])
    last = [local, swapped(local, "core", 1)]
    scale = (own * n_row * peers * 2) ** -0.5

    def finish(*refs):
        finish_kernel(scale, *refs)

    input_grad, weight_grad = pl.pallas_call(
        finish,
        out_shape=[
            jax.ShapeDtypeStruct((own, feat), BF16),
            jax.ShapeDtypeStruct((feat, hid), F32),
        ],
        in_specs=[VMEM] * 3,
        out_specs=[VMEM, VMEM],
        compiler_params=params(16),
        name="finish",
    )(shares, *last)
    return (hidden, input_grad, weight_grad)


def solution(mesh):
    side = 4
    fine = Mesh(
        mesh.devices.reshape(mesh.shape["row"], side, side, 2), ("row", "y", "x", "core")
    )
    col = ("y", "x", "core")
    placed = (
        P((*col, "row"), None),
        P(),
        P("row", col, None, None, None),
        P("row", col, None),
        P("row", col, None),
        P("row", col),
        P(("row", *col), None),
    )
    return jax.shard_map(
        per_device,
        mesh=fine,
        in_specs=placed,
        out_specs=(P(("row", *col), None), P((*col, "row"), None), P()),
        check_vma=False,
    )
```

```python
import jax
import jax.numpy as jnp
from jax import lax
from jax.experimental import pallas as pl
from jax.experimental.pallas import tpu as pltpu
from jax.sharding import Mesh, PartitionSpec as P

F32, BF16, I32 = jnp.float32, jnp.bfloat16, jnp.int32
UNROLL = 16
LIST = 240
WORDS = 512
CHUNKS = 8
AHEAD = 8
NEAR = (1, 7, 2, 6, 3, 5, 4)
SMEM = pl.BlockSpec(memory_space=pltpu.SMEM)
VMEM = pl.BlockSpec(memory_space=pltpu.VMEM)
HBM = pl.BlockSpec(memory_space=pltpu.HBM)


def params(mebibytes):
    return pltpu.CompilerParams(vmem_limit_bytes=mebibytes * 2**20)


def stacked(shape, *rows):
    spot = lax.broadcasted_iota(I32, shape, 0)
    out = jnp.zeros(shape, F32)
    for index, row in enumerate(rows):
        out = jnp.where(spot == index, row.astype(F32), out)
    return out.astype(BF16)


def ones_where(mask):
    return jnp.where(mask, 1.0, 0.0).astype(BF16)


def over_lanes(left, right):
    return lax.dot_general(left, right, (((1,), (1,)), ((), ())), preferred_element_type=F32)


def write_list(key, own, bins, part_of_bin, target, source, source_at, slot, valid, earlier, words):
    slots, width = slot.shape[1], words.shape[1]
    member = jnp.logical_and(lax.broadcasted_iota(I32, (bins, slots), 0) == key, valid)
    before = jnp.dot(
        ones_where(member), earlier[:slots, :slots], preferred_element_type=F32
    )
    rank = jnp.sum(jnp.where(member, before, 0.0), axis=0, keepdims=True).astype(I32)
    name = jnp.where(valid, (rank >> 1) * bins + key, -1)
    named = lax.broadcasted_iota(I32, (width, slots), 0) == name
    closes = (rank & 1) == 1
    closing = [jnp.logical_and(jnp.logical_and(closes, valid), own == index) for index in range(2)]
    marks = stacked((8, slots), *[jnp.where(mask, 1.0, 0.0) for mask in closing])
    ahead = jnp.dot(marks, earlier[:slots, :slots], preferred_element_type=F32)
    turn = jnp.where(own == 1, ahead[1:2], ahead[0:1])
    fields = stacked(
        (8, slots), slot >> 1, slot & 1, source, target, jnp.ones_like(slot), turn
    )
    opened = over_lanes(fields, ones_where(jnp.logical_and(named, jnp.logical_not(closes))))
    closed = over_lanes(fields, ones_where(jnp.logical_and(named, closes)))
    lane = lax.broadcasted_iota(I32, (1, width), 1)
    part = part_of_bin(lane & (bins - 1))
    used, paired = opened[4:5] > 0.5, closed[4:5] > 0.5
    masks = [jnp.logical_and(used, part == index) for index in range(2)]
    singles = [jnp.logical_and(mask, jnp.logical_not(paired)) for mask in masks]
    marks = stacked((8, width), *[jnp.where(mask, 1.0, 0.0) for mask in singles])
    ahead = jnp.dot(marks, earlier, preferred_element_type=F32)
    place = jnp.full((1, width), -1, I32)
    for index, (mask, single) in enumerate(zip(masks, singles)):
        couples = jnp.where(jnp.logical_and(mask, paired), 1.0, 0.0)
        alone = jnp.sum(couples, axis=1, keepdims=True) + ahead[index : index + 1]
        spot = jnp.where(single, alone, closed[5:6]).astype(I32) + index * LIST
        place = jnp.where(mask, spot, place)
    other = [jnp.where(paired, closed[index : index + 1], opened[index : index + 1]) for index in range(3)]
    fields = stacked((8, width), *[opened[index : index + 1] for index in range(4)], *other)
    moved = over_lanes(
        fields, ones_where(lax.broadcasted_iota(I32, (width, width), 0) == place)
    ).astype(I32)
    high, low, source_a, target, high_b, low_b, source_b = [moved[k : k + 1] for k in range(7)]
    word = 2 * high + low + ((2 * high_b + low_b) << 9)
    word = word + (target << 18) + (source_a << source_at) + (source_b << 27)
    for index, mask in enumerate(masks):
        length = jnp.sum(jnp.where(mask, 1.0, 0.0), axis=1, keepdims=True).astype(I32)
        word = jnp.where(lane == width - 2 + index, length, word)
    words[...] = word


def prepare_kernel(rows, cols, count, forward_words, backward_words, padded):
    core = lax.axis_index("core")
    padded[...] = jnp.zeros_like(padded)
    padded[0:1, : rows.shape[2]] = rows[0]
    padded[1:2, : rows.shape[2]] = cols[0]
    row, col = padded[0:1], padded[1:2]
    slot = lax.broadcasted_iota(I32, row.shape, 1)
    valid = slot < count[0, 0]
    width = forward_words.shape[1]
    earlier = ones_where(
        lax.broadcasted_iota(I32, (width, width), 0) < lax.broadcasted_iota(I32, (width, width), 1)
    )
    own = jnp.where(((row >> 1) & 1) == core, 1, 0)
    local = ((row >> 2) << 1) + (row & 1)
    shared = (slot, valid, earlier)

    def forward_part(row):
        return jnp.where(((row >> 1) & 1) == core, 1, 0)

    def backward_part(place):
        return 1 - (place & 1)

    write_list(row, own, 64, forward_part, local, col, 23, *shared, forward_words)
    write_list((col << 1) + own, 1 - own, 32, backward_part, col, local, 22, *shared, backward_words)


def weight_of(word, spot, total):
    alone = (word & 511) == ((word >> 9) & 511)
    return jnp.where(spot < total, jnp.where(alone, 0.5, 1.0), 0.0)


def tile_copy(chunk, stored, tiles, sems):
    span = tiles.shape[0] // CHUNKS
    spot = pl.ds(chunk * span, span)
    return pltpu.make_async_copy(stored.at[0, 0, spot], tiles.at[spot], sems.at[chunk])


def start_tiles(chunk, live, stored, tiles, sems):
    span = tiles.shape[0] // CHUNKS

    @pl.when(chunk * span < live)
    def _():
        tile_copy(chunk, stored, tiles, sems).start()


def await_tiles(first, last, live, stored, tiles, sems):
    def body(chunk, carry):
        tile_copy(chunk, stored, tiles, sems).wait()
        start_tiles(chunk + AHEAD, live, stored, tiles, sems)
        return carry

    lax.fori_loop(first, last, body, 0)


def tile_pass(part, words, tiles, multiply, acc, count=None, stored=None, sems=None):
    total = words[0, words.shape[1] - 2 + part]

    def group(step, loaded):
        listed = [words[0, part * LIST + step * UNROLL + offset] for offset in range(UNROLL)]
        if stored is not None:
            span = tiles.shape[0] // CHUNKS
            highest = 0
            for word in listed:
                highest = jnp.maximum(highest, (word >> 9) & 511)
            needed = jnp.maximum(loaded, highest // span + 1)
            await_tiles(loaded, needed, count[0, 0], stored, tiles, sems)
            loaded = needed
        results = []
        for offset, word in enumerate(listed):
            target, product = multiply(word, tiles)
            weight = weight_of(word, step * UNROLL + offset, total)
            results.append((target, product * weight))
        for target, product in results:
            acc[target] += product
        return loaded

    loaded = lax.fori_loop(0, pl.cdiv(total, UNROLL), group, 0)
    if stored is not None:
        span = tiles.shape[0] // CHUNKS
        await_tiles(loaded, pl.cdiv(count[0, 0], span), count[0, 0], stored, tiles, sems)


def forward_product(panel):
    def multiply(word, tiles):
        pair = jnp.concatenate([tiles[word & 511], tiles[(word >> 9) & 511]], axis=1)
        source = jnp.concatenate([panel[(word >> 23) & 15], panel[(word >> 27) & 15]], axis=0)
        return (word >> 18) & 31, jnp.dot(pair, source, preferred_element_type=F32)

    return multiply


def backward_product(grads):
    def multiply(word, tiles):
        pair = jnp.concatenate([tiles[word & 511], tiles[(word >> 9) & 511]], axis=0)
        source = jnp.concatenate([grads[(word >> 22) & 31], grads[(word >> 27) & 31]], axis=0)
        product = lax.dot_general(
            pair, source, (((0,), (0,)), ((), ())), preferred_element_type=F32
        )
        return (word >> 18) & 15, product

    return multiply


def forward_send_kernel(words, tiles, *refs):
    *blocks, send, panel, acc = refs
    here, rows = lax.axis_index("row"), lax.axis_size("row")
    size = panel.shape[1]
    for distance, block in zip((0, *NEAR), blocks):
        owner = lax.rem(here - distance + rows, rows)
        for part in range(block.shape[0] // size):
            panel[2 * owner + part] = block[pl.ds(part * size, size)]
    acc[...] = jnp.zeros_like(acc)
    tile_pass(0, words, tiles, forward_product(panel), acc)
    send[...] = acc[...].astype(BF16)


def forward_keep_kernel(words, tiles, panel, keep):
    keep[...] = jnp.zeros_like(keep)
    tile_pass(1, words, tiles, forward_product(panel), keep)


def middle_kernel(parts, weight, cotangent, hidden, payload, keep, send):
    peers = parts.shape[0]
    feat = weight.shape[0]
    agg = parts[0].astype(F32)
    for peer in range(1, peers):
        agg += parts[peer].astype(F32)
    high = agg.astype(BF16)
    rest = agg - high.astype(F32)
    low = rest.astype(BF16)
    lowest = (rest - low.astype(F32)).astype(BF16)
    pre = sum(jnp.dot(term, weight[...], preferred_element_type=F32) for term in (lowest, low, high))
    slope, cubic = 0.7978845608028654, 0.044715
    square = pre * pre
    curve = jnp.tanh(slope * pre * (1.0 + cubic * square))
    cdf = 0.5 * (1.0 + curve)
    hidden[...] = (pre * cdf).astype(BF16)
    rate = cdf + 0.5 * pre * (1.0 - curve * curve) * (slope * (1.0 + 3.0 * cubic * square))
    act = cotangent[...].astype(F32) * rate
    grad = lax.dot_general(
        act.astype(BF16), weight[...], (((1,), (1,)), ((), ())), preferred_element_type=F32
    ).astype(BF16)
    for peer in range(peers):
        payload[peer] = grad
    share = lax.dot_general(
        high, act.astype(BF16), (((0,), (0,)), ((), ())), preferred_element_type=F32
    ).astype(BF16)
    first = lax.axis_index("core") == 0
    keep[...] = jnp.where(first, share[:, :feat], share[:, feat:])
    send[...] = jnp.where(first, share[:, feat:], share[:, :feat])


def backward_first_kernel(words, count, stored, grads, acc, tiles, sems):
    for chunk in range(AHEAD):
        start_tiles(chunk, count[0, 0], stored, tiles, sems)
    acc[...] = jnp.zeros_like(acc)
    tile_pass(0, words, tiles, backward_product(grads), acc, count, stored, sems)


def backward_second_kernel(words, tiles, grads, start, out, acc):
    acc[...] = start[...]
    tile_pass(1, words, tiles, backward_product(grads), acc)
    per_peer = out.shape[1] // acc.shape[1]
    for peer in range(out.shape[0]):
        for part in range(per_peer):
            spot = pl.ds(part * acc.shape[1], acc.shape[1])
            out[peer, spot] = acc[peer * per_peer + part].astype(BF16)


def finish_kernel(scale, parts, mine, other, grad, weight_grad):
    total = parts[0].astype(F32)
    for peer in range(1, parts.shape[0]):
        total += parts[peer].astype(F32)
    grad[...] = total.astype(BF16)
    feat = grad.shape[1]
    left = lax.axis_index("core") == 0
    weight_grad[:, :feat] = jnp.where(left, mine[...], other[...]).astype(F32) * scale
    weight_grad[:, feat:] = jnp.where(left, other[...], mine[...]).astype(F32) * scale


def add_kernel(*refs):
    *terms, total = refs
    total[...] = added(*[term[...] for term in terms]).astype(BF16)


def summed(*terms):
    return pl.pallas_call(
        add_kernel,
        out_shape=jax.ShapeDtypeStruct(terms[0].shape, BF16),
        in_specs=[VMEM] * len(terms),
        out_specs=VMEM,
        compiler_params=params(4),
        name="add",
    )(*terms)


def added(*terms):
    terms = [term.astype(F32) for term in terms]
    while len(terms) > 1:
        terms = [left + right for left, right in zip(terms[::2], terms[1::2])]
    return terms[0]


def swapped(value, axis, step):
    return lax.ppermute(value, axis, [(i, i ^ step) for i in range(lax.axis_size(axis))])


def shifted(value, axis, step):
    size = lax.axis_size(axis)
    return lax.ppermute(value, axis, [(i, (i + step) % size) for i in range(size)])


def per_device(features, weight, adj_tiles, tile_rows, tile_cols, tile_count, cotangent):
    own, feat = features.shape
    hid = weight.shape[1]
    n_row = lax.axis_size("row")
    peers = lax.axis_size("y") * lax.axis_size("x")
    slots, size = adj_tiles.shape[2], adj_tiles.shape[-1]
    half_rows = own * peers // size
    col_tiles = own * n_row // size
    yx = ("y", "x")

    stored = pltpu.with_memory_space_constraint(adj_tiles, pltpu.HBM)
    held = pltpu.VMEM((slots, size, size), BF16)
    list_shape = jax.ShapeDtypeStruct((1, WORDS), I32)
    forward_words, backward_words = pl.pallas_call(
        prepare_kernel,
        out_shape=[list_shape, list_shape],
        in_specs=[VMEM, VMEM, SMEM],
        out_specs=[VMEM, VMEM],
        scratch_shapes=[pltpu.VMEM((8, -(-slots // 128) * 128), I32)],
        compiler_params=params(16),
        cost_estimate=pl.CostEstimate(flops=10**10, bytes_accessed=0, transcendentals=0),
        name="prepare",
    )(
        *[pltpu.with_memory_space_constraint(v, pltpu.HBM) for v in (tile_rows, tile_cols)],
        tile_count,
    )
    resident = pltpu.with_memory_space_constraint(
        adj_tiles.reshape(slots, size, size), pltpu.VMEM
    )
    after, before, after2, before2 = [shifted(features, "row", way) for way in NEAR[:4]]
    after3, before3 = shifted(after2, "row", 1), shifted(before2, "row", 7)
    opposite = shifted(after2, "row", 2)
    blocks = (features, after, before, after2, before2, after3, before3, opposite)
    flops = slots * size * size * feat
    tile_cost = pl.CostEstimate(flops=flops, bytes_accessed=adj_tiles.size, transcendentals=0)
    send, panel = pl.pallas_call(
        forward_send_kernel,
        out_shape=[
            jax.ShapeDtypeStruct((half_rows, size, feat), BF16),
            jax.ShapeDtypeStruct((col_tiles, size, feat), BF16),
        ],
        in_specs=[SMEM, VMEM, *([VMEM] * n_row)],
        out_specs=[VMEM, VMEM],
        scratch_shapes=[pltpu.VMEM((half_rows, size, feat), F32)],
        compiler_params=params(16),
        cost_estimate=tile_cost,
        name="forward_send",
    )(forward_words, resident, *blocks)
    got = swapped(send, "core", 1)
    keep = pl.pallas_call(
        forward_keep_kernel,
        out_shape=jax.ShapeDtypeStruct((half_rows, size, feat), F32),
        in_specs=[SMEM, VMEM, VMEM],
        out_specs=VMEM,
        compiler_params=params(16),
        cost_estimate=tile_cost,
        name="forward_keep",
    )(forward_words, resident, panel)
    paired = (keep + got.astype(F32)).astype(BF16).reshape(peers, own, feat)
    parts = lax.all_to_all(paired, yx, 0, 0, tiled=True)
    hidden, payload, local, given = pl.pallas_call(
        middle_kernel,
        out_shape=[
            jax.ShapeDtypeStruct(cotangent.shape, BF16),
            jax.ShapeDtypeStruct((peers, own, feat), BF16),
            jax.ShapeDtypeStruct((feat, hid // 2), BF16),
            jax.ShapeDtypeStruct((feat, hid // 2), BF16),
        ],
        in_specs=[VMEM, VMEM, VMEM],
        out_specs=[VMEM, VMEM, VMEM, VMEM],
        compiler_params=params(16),
        name="middle",
    )(parts, weight, cotangent)

    local = added(local, swapped(given, "core", 1)).astype(BF16)
    local = added(local, swapped(local, "row", 1)).astype(BF16)
    local = added(local, *[shifted(local, "row", step) for step in (4, 2, 6)]).astype(BF16)
    mine = lax.all_to_all(payload, yx, 0, 0, tiled=True).reshape(half_rows, size, feat)
    mine, local = lax.optimization_barrier((mine, local))
    other = swapped(mine, "core", 1)
    beside = swapped(local, "x", 1)
    started, tiles = pl.pallas_call(
        backward_first_kernel,
        out_shape=[jax.ShapeDtypeStruct((col_tiles, size, feat), F32), held],
        in_specs=[SMEM, SMEM, HBM, VMEM],
        out_specs=[VMEM, VMEM],
        scratch_shapes=[pltpu.SemaphoreType.DMA((CHUNKS,))],
        compiler_params=params(16),
        cost_estimate=tile_cost,
        name="backward_first",
    )(backward_words, tile_count, stored, mine)
    col_partial = pl.pallas_call(
        backward_second_kernel,
        out_shape=jax.ShapeDtypeStruct((n_row, own, feat), BF16),
        in_specs=[SMEM, VMEM, VMEM, VMEM],
        out_specs=VMEM,
        scratch_shapes=[pltpu.VMEM((col_tiles, size, feat), F32)],
        compiler_params=params(16),
        cost_estimate=tile_cost,
        name="backward_second",
    )(backward_words, tiles, other, started)
    col_partial, local, beside = lax.optimization_barrier((col_partial, local, beside))
    shares = lax.all_to_all(col_partial, "row", 0, 0, tiled=True)
    local = summed(local, beside)
    local = summed(local, swapped(local, "x", 2))
    local = summed(local, *[shifted(local, "y", step) for step in (2, 1, 3)])
    last = [local, swapped(local, "core", 1)]
    scale = (own * n_row * peers * 2) ** -0.5

    def finish(*refs):
        finish_kernel(scale, *refs)

    input_grad, weight_grad = pl.pallas_call(
        finish,
        out_shape=[
            jax.ShapeDtypeStruct((own, feat), BF16),
            jax.ShapeDtypeStruct((feat, hid), F32),
        ],
        in_specs=[VMEM] * 3,
        out_specs=[VMEM, VMEM],
        compiler_params=params(16),
        name="finish",
    )(shares, *last)
    return (hidden, input_grad, weight_grad)


def solution(mesh):
    side = 4
    fine = Mesh(
        mesh.devices.reshape(mesh.shape["row"], side, side, 2), ("row", "y", "x", "core")
    )
    col = ("y", "x", "core")
    placed = (
        P((*col, "row"), None),
        P(),
        P("row", col, None, None, None),
        P("row", col, None),
        P("row", col, None),
        P("row", col),
        P(("row", *col), None),
    )
    return jax.shard_map(
        per_device,
        mesh=fine,
        in_specs=placed,
        out_specs=(P(("row", *col), None), P((*col, "row"), None), P()),
        check_vma=False,
    )
```

```python
import jax
import jax.numpy as jnp
from jax import lax
from jax.experimental import pallas as pl
from jax.experimental.pallas import tpu as pltpu
from jax.sharding import Mesh, PartitionSpec as P

F32, BF16, I32 = jnp.float32, jnp.bfloat16, jnp.int32
UNROLL = 16
LIST = 240
WORDS = 512
CHUNKS = 16
AHEAD = 16
NEAR = (1, 7, 2, 6, 3, 5, 4)
SMEM = pl.BlockSpec(memory_space=pltpu.SMEM)
VMEM = pl.BlockSpec(memory_space=pltpu.VMEM)
HBM = pl.BlockSpec(memory_space=pltpu.HBM)


def params(mebibytes):
    return pltpu.CompilerParams(vmem_limit_bytes=mebibytes * 2**20)


def stacked(shape, *rows):
    spot = lax.broadcasted_iota(I32, shape, 0)
    out = jnp.zeros(shape, F32)
    for index, row in enumerate(rows):
        out = jnp.where(spot == index, row.astype(F32), out)
    return out.astype(BF16)


def ones_where(mask):
    return jnp.where(mask, 1.0, 0.0).astype(BF16)


def over_lanes(left, right):
    return lax.dot_general(left, right, (((1,), (1,)), ((), ())), preferred_element_type=F32)


def write_list(key, own, bins, part_of_bin, target, source, source_at, slot, valid, earlier, words):
    slots, width = slot.shape[1], words.shape[1]
    member = jnp.logical_and(lax.broadcasted_iota(I32, (bins, slots), 0) == key, valid)
    before = jnp.dot(
        ones_where(member), earlier[:slots, :slots], preferred_element_type=F32
    )
    rank = jnp.sum(jnp.where(member, before, 0.0), axis=0, keepdims=True).astype(I32)
    name = jnp.where(valid, (rank >> 1) * bins + key, -1)
    named = lax.broadcasted_iota(I32, (width, slots), 0) == name
    closes = (rank & 1) == 1
    closing = [jnp.logical_and(jnp.logical_and(closes, valid), own == index) for index in range(2)]
    marks = stacked((8, slots), *[jnp.where(mask, 1.0, 0.0) for mask in closing])
    ahead = jnp.dot(marks, earlier[:slots, :slots], preferred_element_type=F32)
    turn = jnp.where(own == 1, ahead[1:2], ahead[0:1])
    fields = stacked(
        (8, slots), slot >> 1, slot & 1, source, target, jnp.ones_like(slot), turn
    )
    opened = over_lanes(fields, ones_where(jnp.logical_and(named, jnp.logical_not(closes))))
    closed = over_lanes(fields, ones_where(jnp.logical_and(named, closes)))
    lane = lax.broadcasted_iota(I32, (1, width), 1)
    part = part_of_bin(lane & (bins - 1))
    used, paired = opened[4:5] > 0.5, closed[4:5] > 0.5
    masks = [jnp.logical_and(used, part == index) for index in range(2)]
    singles = [jnp.logical_and(mask, jnp.logical_not(paired)) for mask in masks]
    marks = stacked((8, width), *[jnp.where(mask, 1.0, 0.0) for mask in singles])
    ahead = jnp.dot(marks, earlier, preferred_element_type=F32)
    place = jnp.full((1, width), -1, I32)
    for index, (mask, single) in enumerate(zip(masks, singles)):
        couples = jnp.where(jnp.logical_and(mask, paired), 1.0, 0.0)
        alone = jnp.sum(couples, axis=1, keepdims=True) + ahead[index : index + 1]
        spot = jnp.where(single, alone, closed[5:6]).astype(I32) + index * LIST
        place = jnp.where(mask, spot, place)
    other = [jnp.where(paired, closed[index : index + 1], opened[index : index + 1]) for index in range(3)]
    fields = stacked((8, width), *[opened[index : index + 1] for index in range(4)], *other)
    moved = over_lanes(
        fields, ones_where(lax.broadcasted_iota(I32, (width, width), 0) == place)
    ).astype(I32)
    high, low, source_a, target, high_b, low_b, source_b = [moved[k : k + 1] for k in range(7)]
    word = 2 * high + low + ((2 * high_b + low_b) << 9)
    word = word + (target << 18) + (source_a << source_at) + (source_b << 27)
    for index, mask in enumerate(masks):
        length = jnp.sum(jnp.where(mask, 1.0, 0.0), axis=1, keepdims=True).astype(I32)
        word = jnp.where(lane == width - 2 + index, length, word)
    words[...] = word


def prepare_kernel(rows, cols, count, forward_words, backward_words, padded, *scratch):
    row_block, col_block, row_sem, col_sem = scratch
    loads = [
        pltpu.make_async_copy(rows, row_block, row_sem),
        pltpu.make_async_copy(cols, col_block, col_sem),
    ]
    for load in loads:
        load.start()
    core = lax.axis_index("core")
    width = forward_words.shape[1]
    earlier = ones_where(
        lax.broadcasted_iota(I32, (width, width), 0) < lax.broadcasted_iota(I32, (width, width), 1)
    )
    padded[...] = jnp.zeros_like(padded)
    for load in loads:
        load.wait()
    padded[0:1, : rows.shape[2]] = row_block[0]
    padded[1:2, : rows.shape[2]] = col_block[0]
    row, col = padded[0:1], padded[1:2]
    slot = lax.broadcasted_iota(I32, row.shape, 1)
    valid = slot < count[0, 0]
    own = jnp.where(((row >> 1) & 1) == core, 1, 0)
    local = ((row >> 2) << 1) + (row & 1)
    shared = (slot, valid, earlier)

    def forward_part(row):
        return jnp.where(((row >> 1) & 1) == core, 1, 0)

    def backward_part(place):
        return 1 - (place & 1)

    write_list(row, own, 64, forward_part, local, col, 23, *shared, forward_words)
    write_list((col << 1) + own, 1 - own, 32, backward_part, col, local, 22, *shared, backward_words)


def weight_of(word, spot, total):
    alone = (word & 511) == ((word >> 9) & 511)
    return jnp.where(spot < total, jnp.where(alone, 0.5, 1.0), 0.0)


def tile_copy(chunk, stored, tiles, sems):
    span = tiles.shape[0] // CHUNKS
    spot = pl.ds(chunk * span, span)
    return pltpu.make_async_copy(stored.at[0, 0, spot], tiles.at[spot], sems.at[chunk])


def start_tiles(chunk, live, stored, tiles, sems):
    span = tiles.shape[0] // CHUNKS

    @pl.when(chunk * span < live)
    def _():
        tile_copy(chunk, stored, tiles, sems).start()


def await_tiles(first, last, live, stored, tiles, sems):
    def body(chunk, carry):
        tile_copy(chunk, stored, tiles, sems).wait()
        start_tiles(chunk + AHEAD, live, stored, tiles, sems)
        return carry

    lax.fori_loop(first, last, body, 0)


def tile_pass(part, words, tiles, multiply, acc, count=None, stored=None, sems=None):
    total = words[0, words.shape[1] - 2 + part]

    def group(step, loaded):
        listed = [words[0, part * LIST + step * UNROLL + offset] for offset in range(UNROLL)]
        if stored is not None:
            span = tiles.shape[0] // CHUNKS
            highest = 0
            for word in listed:
                highest = jnp.maximum(highest, (word >> 9) & 511)
            needed = jnp.maximum(loaded, highest // span + 1)
            await_tiles(loaded, needed, count[0, 0], stored, tiles, sems)
            loaded = needed
        results = []
        for offset, word in enumerate(listed):
            target, product = multiply(word, tiles)
            weight = weight_of(word, step * UNROLL + offset, total)
            results.append((target, product * weight))
        for target, product in results:
            acc[target] += product
        return loaded

    loaded = lax.fori_loop(0, pl.cdiv(total, UNROLL), group, 0)
    if stored is not None:
        span = tiles.shape[0] // CHUNKS
        await_tiles(loaded, pl.cdiv(count[0, 0], span), count[0, 0], stored, tiles, sems)


def forward_product(panel):
    def multiply(word, tiles):
        pair = jnp.concatenate([tiles[word & 511], tiles[(word >> 9) & 511]], axis=1)
        source = jnp.concatenate([panel[(word >> 23) & 15], panel[(word >> 27) & 15]], axis=0)
        return (word >> 18) & 31, jnp.dot(pair, source, preferred_element_type=F32)

    return multiply


def backward_product(grads):
    def multiply(word, tiles):
        pair = jnp.concatenate([tiles[word & 511], tiles[(word >> 9) & 511]], axis=0)
        source = jnp.concatenate([grads[(word >> 22) & 31], grads[(word >> 27) & 31]], axis=0)
        product = lax.dot_general(
            pair, source, (((0,), (0,)), ((), ())), preferred_element_type=F32
        )
        return (word >> 18) & 15, product

    return multiply


def forward_send_kernel(words, tiles, *refs):
    *blocks, send, panel, acc = refs
    here, rows = lax.axis_index("row"), lax.axis_size("row")
    size = panel.shape[1]
    for distance, block in zip((0, *NEAR), blocks):
        owner = lax.rem(here - distance + rows, rows)
        for part in range(block.shape[0] // size):
            panel[2 * owner + part] = block[pl.ds(part * size, size)]
    acc[...] = jnp.zeros_like(acc)
    tile_pass(0, words, tiles, forward_product(panel), acc)
    send[...] = acc[...].astype(BF16)


def forward_keep_kernel(words, tiles, panel, keep):
    keep[...] = jnp.zeros_like(keep)
    tile_pass(1, words, tiles, forward_product(panel), keep)


def middle_kernel(parts, weight, cotangent, hidden, payload, keep, send):
    peers = parts.shape[0]
    feat = weight.shape[0]
    agg = parts[0].astype(F32)
    for peer in range(1, peers):
        agg += parts[peer].astype(F32)
    high = agg.astype(BF16)
    rest = agg - high.astype(F32)
    low = rest.astype(BF16)
    lowest = (rest - low.astype(F32)).astype(BF16)
    pre = sum(jnp.dot(term, weight[...], preferred_element_type=F32) for term in (lowest, low, high))
    slope, cubic = 0.7978845608028654, 0.044715
    square = pre * pre
    curve = jnp.tanh(slope * pre * (1.0 + cubic * square))
    cdf = 0.5 * (1.0 + curve)
    hidden[...] = (pre * cdf).astype(BF16)
    rate = cdf + 0.5 * pre * (1.0 - curve * curve) * (slope * (1.0 + 3.0 * cubic * square))
    act = cotangent[...].astype(F32) * rate
    grad = lax.dot_general(
        act.astype(BF16), weight[...], (((1,), (1,)), ((), ())), preferred_element_type=F32
    ).astype(BF16)
    for peer in range(peers):
        payload[peer] = grad
    share = lax.dot_general(
        high, act.astype(BF16), (((0,), (0,)), ((), ())), preferred_element_type=F32
    ).astype(BF16)
    first = lax.axis_index("core") == 0
    keep[...] = jnp.where(first, share[:, :feat], share[:, feat:])
    send[...] = jnp.where(first, share[:, feat:], share[:, :feat])


def backward_first_kernel(words, count, stored, grads, acc, tiles, sems):
    for chunk in range(AHEAD):
        start_tiles(chunk, count[0, 0], stored, tiles, sems)
    acc[...] = jnp.zeros_like(acc)
    tile_pass(0, words, tiles, backward_product(grads), acc, count, stored, sems)


def backward_second_kernel(words, tiles, grads, start, out, acc):
    acc[...] = start[...]
    tile_pass(1, words, tiles, backward_product(grads), acc)
    per_peer = out.shape[1] // acc.shape[1]
    for peer in range(out.shape[0]):
        for part in range(per_peer):
            spot = pl.ds(part * acc.shape[1], acc.shape[1])
            out[peer, spot] = acc[peer * per_peer + part].astype(BF16)


def finish_kernel(scale, parts, mine, other, grad, weight_grad):
    total = parts[0].astype(F32)
    for peer in range(1, parts.shape[0]):
        total += parts[peer].astype(F32)
    grad[...] = total.astype(BF16)
    feat = grad.shape[1]
    left = lax.axis_index("core") == 0
    weight_grad[:, :feat] = jnp.where(left, mine[...], other[...]).astype(F32) * scale
    weight_grad[:, feat:] = jnp.where(left, other[...], mine[...]).astype(F32) * scale


def add_kernel(*refs):
    *terms, total = refs
    total[...] = added(*[term[...] for term in terms]).astype(BF16)


def summed(*terms):
    return pl.pallas_call(
        add_kernel,
        out_shape=jax.ShapeDtypeStruct(terms[0].shape, BF16),
        in_specs=[VMEM] * len(terms),
        out_specs=VMEM,
        compiler_params=params(4),
        name="add",
    )(*terms)


def added(*terms):
    terms = [term.astype(F32) for term in terms]
    while len(terms) > 1:
        terms = [left + right for left, right in zip(terms[::2], terms[1::2])]
    return terms[0]


def swapped(value, axis, step):
    return lax.ppermute(value, axis, [(i, i ^ step) for i in range(lax.axis_size(axis))])


def shifted(value, axis, step):
    size = lax.axis_size(axis)
    return lax.ppermute(value, axis, [(i, (i + step) % size) for i in range(size)])


def per_device(features, weight, adj_tiles, tile_rows, tile_cols, tile_count, cotangent):
    own, feat = features.shape
    hid = weight.shape[1]
    n_row = lax.axis_size("row")
    peers = lax.axis_size("y") * lax.axis_size("x")
    slots, size = adj_tiles.shape[2], adj_tiles.shape[-1]
    half_rows = own * peers // size
    col_tiles = own * n_row // size
    yx = ("y", "x")

    stored = pltpu.with_memory_space_constraint(adj_tiles, pltpu.HBM)
    held = pltpu.VMEM((slots, size, size), BF16)
    list_shape = jax.ShapeDtypeStruct((1, WORDS), I32)
    forward_words, backward_words = pl.pallas_call(
        prepare_kernel,
        out_shape=[list_shape, list_shape],
        in_specs=[HBM, HBM, SMEM],
        out_specs=[VMEM, VMEM],
        scratch_shapes=[
            pltpu.VMEM((8, -(-slots // 128) * 128), I32),
            pltpu.VMEM(tile_rows.shape, I32),
            pltpu.VMEM(tile_cols.shape, I32),
            pltpu.SemaphoreType.DMA(()),
            pltpu.SemaphoreType.DMA(()),
        ],
        compiler_params=params(16),
        cost_estimate=pl.CostEstimate(flops=10**10, bytes_accessed=0, transcendentals=0),
        name="prepare",
    )(
        *[pltpu.with_memory_space_constraint(v, pltpu.HBM) for v in (tile_rows, tile_cols)],
        tile_count,
    )
    resident = pltpu.with_memory_space_constraint(
        adj_tiles.reshape(slots, size, size), pltpu.VMEM
    )
    after, before, after2, before2 = [shifted(features, "row", way) for way in NEAR[:4]]
    after3, before3 = shifted(after2, "row", 1), shifted(before2, "row", 7)
    opposite = shifted(after2, "row", 2)
    blocks = (features, after, before, after2, before2, after3, before3, opposite)
    flops = slots * size * size * feat
    tile_cost = pl.CostEstimate(flops=flops, bytes_accessed=adj_tiles.size, transcendentals=0)
    send, panel = pl.pallas_call(
        forward_send_kernel,
        out_shape=[
            jax.ShapeDtypeStruct((half_rows, size, feat), BF16),
            jax.ShapeDtypeStruct((col_tiles, size, feat), BF16),
        ],
        in_specs=[SMEM, VMEM, *([VMEM] * n_row)],
        out_specs=[VMEM, VMEM],
        scratch_shapes=[pltpu.VMEM((half_rows, size, feat), F32)],
        compiler_params=params(16),
        cost_estimate=tile_cost,
        name="forward_send",
    )(forward_words, resident, *blocks)
    got = swapped(send, "core", 1)
    keep = pl.pallas_call(
        forward_keep_kernel,
        out_shape=jax.ShapeDtypeStruct((half_rows, size, feat), F32),
        in_specs=[SMEM, VMEM, VMEM],
        out_specs=VMEM,
        compiler_params=params(16),
        cost_estimate=tile_cost,
        name="forward_keep",
    )(forward_words, resident, panel)
    paired = (keep + got.astype(F32)).astype(BF16).reshape(peers, own, feat)
    parts = lax.all_to_all(paired, yx, 0, 0, tiled=True)
    hidden, payload, local, given = pl.pallas_call(
        middle_kernel,
        out_shape=[
            jax.ShapeDtypeStruct(cotangent.shape, BF16),
            jax.ShapeDtypeStruct((peers, own, feat), BF16),
            jax.ShapeDtypeStruct((feat, hid // 2), BF16),
            jax.ShapeDtypeStruct((feat, hid // 2), BF16),
        ],
        in_specs=[VMEM, VMEM, VMEM],
        out_specs=[VMEM, VMEM, VMEM, VMEM],
        compiler_params=params(16),
        name="middle",
    )(parts, weight, cotangent)

    local = added(local, swapped(given, "core", 1)).astype(BF16)
    local = added(local, swapped(local, "row", 1)).astype(BF16)
    local = added(local, *[shifted(local, "row", step) for step in (4, 2, 6)]).astype(BF16)
    mine = lax.all_to_all(payload, yx, 0, 0, tiled=True).reshape(half_rows, size, feat)
    mine, local = lax.optimization_barrier((mine, local))
    other = swapped(mine, "core", 1)
    beside = swapped(local, "x", 1)
    started, tiles = pl.pallas_call(
        backward_first_kernel,
        out_shape=[jax.ShapeDtypeStruct((col_tiles, size, feat), F32), held],
        in_specs=[SMEM, SMEM, HBM, VMEM],
        out_specs=[VMEM, VMEM],
        scratch_shapes=[pltpu.SemaphoreType.DMA((CHUNKS,))],
        compiler_params=params(16),
        cost_estimate=tile_cost,
        name="backward_first",
    )(backward_words, tile_count, stored, mine)
    col_partial = pl.pallas_call(
        backward_second_kernel,
        out_shape=jax.ShapeDtypeStruct((n_row, own, feat), BF16),
        in_specs=[SMEM, VMEM, VMEM, VMEM],
        out_specs=VMEM,
        scratch_shapes=[pltpu.VMEM((col_tiles, size, feat), F32)],
        compiler_params=params(16),
        cost_estimate=tile_cost,
        name="backward_second",
    )(backward_words, tiles, other, started)
    col_partial, local, beside = lax.optimization_barrier((col_partial, local, beside))
    shares = lax.all_to_all(col_partial, "row", 0, 0, tiled=True)
    local = summed(local, beside)
    local = summed(local, swapped(local, "x", 2))
    local = summed(local, *[shifted(local, "y", step) for step in (2, 1, 3)])
    last = [local, swapped(local, "core", 1)]
    scale = (own * n_row * peers * 2) ** -0.5

    def finish(*refs):
        finish_kernel(scale, *refs)

    input_grad, weight_grad = pl.pallas_call(
        finish,
        out_shape=[
            jax.ShapeDtypeStruct((own, feat), BF16),
            jax.ShapeDtypeStruct((feat, hid), F32),
        ],
        in_specs=[VMEM] * 3,
        out_specs=[VMEM, VMEM],
        compiler_params=params(16),
        name="finish",
    )(shares, *last)
    return (hidden, input_grad, weight_grad)


def solution(mesh):
    side = 4
    fine = Mesh(
        mesh.devices.reshape(mesh.shape["row"], side, side, 2), ("row", "y", "x", "core")
    )
    col = ("y", "x", "core")
    placed = (
        P((*col, "row"), None),
        P(),
        P("row", col, None, None, None),
        P("row", col, None),
        P("row", col, None),
        P("row", col),
        P(("row", *col), None),
    )
    return jax.shard_map(
        per_device,
        mesh=fine,
        in_specs=placed,
        out_specs=(P(("row", *col), None), P((*col, "row"), None), P()),
        check_vma=False,
    )
```
